128 devices in a mesh: rep: 8 (over z, y_hi), slab: 16 (over y_lo, x, core).
Axes of the slice: x: 4, y: 4 (y_hi: 2, y_lo: 2; y = y_hi * 2 + y_lo), z: 4, core: 2. Of those that a mesh axis runs over, the one named last changes fastest.
Arguments:
- feats: bfloat16 [8, 32, 24576], P('rep', None, 'slab'), may hold values from -6 to 6
- tile_weight: bfloat16 [8, 1536, 64, 512], P('rep', 'slab'), may hold values from -0.25 to 0.25
- tile_atom: int32 [8, 1536], P('rep', 'slab'), may hold values from 0 to 23
- tile_cell: int32 [8, 1536], P('rep', 'slab'), may hold values from 0 to 31
- tile_live: int32 [8, 16], P('rep', 'slab'), may hold values from 24 to 96, as said below
- w_mix: bfloat16 [32, 32], replicated, may hold values from -1 to 1
- conv_w: bfloat16 [27, 32, 32], replicated, may hold values from -0.21875 to 0.21875
- cotangent: bfloat16 [8, 32, 24576], P('rep', None, 'slab'), may hold values from -6 to 6
Outputs:
- potential: bfloat16 [8, 32, 24576], P('rep', None, 'slab')
- grad_feats: bfloat16 [8, 32, 24576], P('rep', None, 'slab')
- grad_conv: float32 [27, 32, 32], replicated
- grad_mix: float32 [32, 32], replicated
The draws below stay inside these ranges and needn't reach their ends.
Inputs may be any that keep to these rules, and one draw needn't show every extreme that they name: The first tile_live slots of a slab's list are live, the rest are ignored; in every system some slab has all 96 slots live. `tile_atom`: atom block within the tile's own slab. `tile_cell`: cell block within the slab's window of 8 planes that starts 2 planes below the slab.
All inputs are finite; a program needn't handle non-finite values.
Results may differ from the reference program's by a relative error of at most 0.013.
Values may be sent and summed in bfloat16 or wider, within the bound.
A program may use at most 128 MiB of HBM per device.

```python
import math
import jax
import jax.numpy as jnp
from jax import lax

C = 32
GY = 32
GX = 64
ZD = 4
ZH = 2
A_DEV = 1536
TILES_DEV = 96
TILE_A = 64
TILE_C = 512
SYSTEMS = 8
SLABS = 16
NZ = 64
ATOMS = 24576
TILES = 1536
PW = 8
NB = 32
NAB = 24


def draw_tile_live(key, part):
    first_key, second_key = jax.random.split(jax.random.fold_in(key, 7))
    counts = jax.random.randint(first_key, (SYSTEMS, SLABS), TILES_DEV // 4, TILES_DEV + 1)
    chosen = jax.random.randint(second_key, (SYSTEMS, 1), 0, SLABS)
    slab_ids = jnp.arange(SLABS, dtype=jnp.int32)[None, :]
    return jnp.where(slab_ids == chosen, TILES_DEV, counts).astype(jnp.int32)


def place_ends(array, rng, low, largest):
    index_at = [jax.random.randint(jax.random.fold_in(rng, axis), (), 0, length) for axis, length in enumerate(array.shape)]
    longest = array.shape.index(max(array.shape))
    beside = index_at[:longest] + [(index_at[longest] + 1) % array.shape[longest]] + index_at[longest + 1:]
    return array.at[tuple(index_at)].set(low).at[tuple(beside)].set(largest)


def shard_levels(own_key, extent, cuts, smallest, top_value):
    loudness, own = 1.0, jax.random.fold_in(own_key, 6)
    for dim, blocks in cuts:
        draws = jnp.exp(jax.random.uniform(jax.random.fold_in(own, dim), (blocks,), jnp.float32, smallest / len(cuts), top_value / len(cuts)))
        loudness = loudness * jnp.repeat(draws, extent[dim] // blocks).reshape([-1 if axis == dim else 1 for axis in range(len(extent))])
    return loudness


def normal_values(rng, dims, scale, limit, shards=(), kind=jnp.bfloat16):
    factor_of = shard_levels(rng, dims, shards, -0.22, 0.18) if shards else 1.0
    values = jax.random.normal(rng, dims, jnp.float32) * scale * factor_of
    return jnp.minimum(jnp.maximum(values, -limit), limit).astype(kind)


def setup_inputs(seed: int = 0) -> dict:
    streams_of = jax.random.split(jax.random.key(seed), 9)
    feats = normal_values(streams_of[0], (SYSTEMS, C, ATOMS), 1.0, 6.0, ((0, 8), (2, 16)))
    tile_weight = normal_values(streams_of[1], (SYSTEMS, TILES, TILE_A, TILE_C), TILE_C ** -0.5, 0.25, ((0, 8), (1, 16)))
    tile_atom = place_ends(jax.random.randint(streams_of[2], (SYSTEMS, TILES), 0, NAB), jax.random.fold_in(streams_of[2], 1), 0, NAB - 1).astype(jnp.int32)
    tile_cell = place_ends(jax.random.randint(streams_of[3], (SYSTEMS, TILES), 0, NB), jax.random.fold_in(streams_of[3], 1), 0, NB - 1).astype(jnp.int32)
    tile_live = draw_tile_live(jax.random.fold_in(streams_of[8], 71), 0)
    w_mix = normal_values(streams_of[5], (C, C), C ** -0.5, 1.0)
    conv_w = normal_values(streams_of[6], (27, C, C), (27 * C) ** -0.5, 0.21875)
    cotangent = normal_values(streams_of[7], (SYSTEMS, C, ATOMS), 1.0, 6.0, ((0, 8), (2, 16)))
    return dict(feats=feats, tile_weight=tile_weight, tile_atom=tile_atom, tile_cell=tile_cell, tile_live=tile_live, w_mix=w_mix, conv_w=conv_w, cotangent=cotangent)


def shifted_stack(field):
    planes = field.shape[1]
    shaped = field.reshape(C, planes, GY, GX)
    pieces = []
    for row_off in (-1, 0, 1):
        for col_off in (-1, 0, 1):
            rolled = jnp.roll(shaped, (-row_off, -col_off), (2, 3))
            pieces.append(rolled.reshape(C, planes, GY * GX))
    return jnp.concatenate(pieces, axis=0)

def conv_valid(field, kernel_set):
    planes = field.shape[1] - 2
    stacked = shifted_stack(field).astype(jnp.float32)
    result = jnp.zeros((C, planes, GY * GX), jnp.float32)
    for plane_off in range(3):
        kernel = jnp.transpose(kernel_set[plane_off * 9:(plane_off + 1) * 9], (1, 0, 2)).reshape(C, 9 * C)
        result = result + jnp.einsum('ok,kpn->opn', kernel.astype(jnp.float32), stacked[:, plane_off:plane_off + planes])
    return result

def weight_grad(upstream, field):
    planes = upstream.shape[1]
    stacked = shifted_stack(field).astype(jnp.float32)
    collected = []
    for plane_off in range(3):
        product = jnp.einsum('opn,kpn->ok', upstream.astype(jnp.float32), stacked[:, plane_off:plane_off + planes])
        collected.append(jnp.transpose(product.reshape(C, 9, C), (1, 0, 2)))
    return jnp.concatenate(collected, axis=0)

def wrap_planes(field, margin):
    return jnp.concatenate([field[:, NZ - margin:], field, field[:, :margin]], axis=1)

def deposit_slab(source, weights, atom_ids, cell_ids, live_tiles):
    blocks = source.reshape(C, NAB, TILE_A)
    picked = blocks[:, atom_ids]
    product = jnp.einsum('ctk,tkn->tcn', picked.astype(jnp.float32), weights.astype(jnp.float32))
    alive = jnp.arange(TILES_DEV, dtype=jnp.int32) < live_tiles
    product = jnp.where(alive[:, None, None], product, 0.0)
    sums = jax.ops.segment_sum(product, cell_ids, num_segments=NB)
    return jnp.transpose(sums, (1, 0, 2)).reshape(C, PW, GY * GX)

def collect_slab(window, weights, atom_ids, cell_ids, live_tiles):
    blocks = window.reshape(C, NB, TILE_C)
    picked = blocks[:, cell_ids]
    product = jnp.einsum('ctn,tkn->tck', picked.astype(jnp.float32), weights.astype(jnp.float32))
    alive = jnp.arange(TILES_DEV, dtype=jnp.int32) < live_tiles
    product = jnp.where(alive[:, None, None], product, 0.0)
    sums = jax.ops.segment_sum(product, atom_ids, num_segments=NAB)
    return jnp.transpose(sums, (1, 0, 2)).reshape(C, A_DEV)

def spread_mesh(source, weights, atom_ids, cell_ids, live_counts):
    slab_src = jnp.transpose(source.reshape(C, SLABS, A_DEV), (1, 0, 2))
    slab_w = weights.reshape(SLABS, TILES_DEV, TILE_A, TILE_C)
    slab_a = atom_ids.reshape(SLABS, TILES_DEV)
    slab_c = cell_ids.reshape(SLABS, TILES_DEV)
    padded = jnp.zeros((C, NZ + 2 * ZH, GY * GX), jnp.float32)

    def one_slab(carry, inputs):
        slab_index, src_part, w_part, a_part, c_part, live_part = inputs
        window = deposit_slab(src_part, w_part, a_part, c_part, live_part)
        offset = (slab_index * ZD).astype(jnp.int32)
        current = lax.dynamic_slice_in_dim(carry, offset, PW, 1)
        return (lax.dynamic_update_slice_in_dim(carry, current + window, offset, 1), None)
    padded, _ = lax.scan(one_slab, padded, (jnp.arange(SLABS, dtype=jnp.int32), slab_src, slab_w, slab_a, slab_c, live_counts))
    mesh = padded[:, ZH:ZH + NZ]
    mesh = mesh.at[:, :ZH].add(padded[:, NZ + ZH:])
    mesh = mesh.at[:, NZ - ZH:].add(padded[:, :ZH])
    return mesh

def gather_atoms(mesh, weights, atom_ids, cell_ids, live_counts):
    extended = wrap_planes(mesh, ZH)
    slab_w = weights.reshape(SLABS, TILES_DEV, TILE_A, TILE_C)
    slab_a = atom_ids.reshape(SLABS, TILES_DEV)
    slab_c = cell_ids.reshape(SLABS, TILES_DEV)

    def one_slab(inputs):
        slab_index, w_part, a_part, c_part, live_part = inputs
        offset = (slab_index * ZD).astype(jnp.int32)
        window = lax.dynamic_slice_in_dim(extended, offset, PW, 1)
        return collect_slab(window, w_part, a_part, c_part, live_part)
    result = lax.map(one_slab, (jnp.arange(SLABS, dtype=jnp.int32), slab_w, slab_a, slab_c, live_counts))
    return jnp.transpose(result, (1, 0, 2)).reshape(C, ATOMS)

def reference(feats, tile_weight, tile_atom, tile_cell, tile_live, w_mix, conv_w, cotangent):
    kernel_flip = jnp.transpose(conv_w[::-1], (0, 2, 1))

    def one_system(inputs):
        atom_feats, weights, atom_ids, cell_ids, live_counts, upstream = inputs
        mixed = jnp.dot(w_mix, atom_feats, preferred_element_type=jnp.float32).astype(jnp.bfloat16)
        density = spread_mesh(mixed, weights, atom_ids, cell_ids, live_counts).astype(jnp.bfloat16)
        field_mesh = conv_valid(wrap_planes(density, 1), conv_w).astype(jnp.bfloat16)
        potential = gather_atoms(field_mesh, weights, atom_ids, cell_ids, live_counts).astype(jnp.bfloat16)
        mesh_grad = spread_mesh(upstream, weights, atom_ids, cell_ids, live_counts).astype(jnp.bfloat16)
        conv_part = weight_grad(mesh_grad, wrap_planes(density, 1))
        density_grad = conv_valid(wrap_planes(mesh_grad, 1), kernel_flip).astype(jnp.bfloat16)
        mixed_grad = gather_atoms(density_grad, weights, atom_ids, cell_ids, live_counts).astype(jnp.bfloat16)
        feats_grad = jnp.dot(w_mix.T, mixed_grad, preferred_element_type=jnp.float32).astype(jnp.bfloat16)
        mix_part = jnp.dot(mixed_grad, atom_feats.T, preferred_element_type=jnp.float32)
        return (potential, feats_grad, conv_part, mix_part)
    potential, feats_grad, conv_parts, mix_parts = lax.map(one_system, (feats, tile_weight, tile_atom, tile_cell, tile_live, cotangent))
    grad_conv = lax.optimization_barrier(jnp.sum(conv_parts, axis=0)) / math.sqrt(SYSTEMS * NZ * GY * GX)
    grad_mix = lax.optimization_barrier(jnp.sum(mix_parts, axis=0)) / math.sqrt(SYSTEMS * ATOMS)
    return (potential, feats_grad, grad_conv, grad_mix)
```

```python
import math

import jax
import jax.numpy as jnp
from jax import lax
from jax.experimental import pallas as pl
from jax.experimental.pallas import tpu as pltpu
from jax.sharding import PartitionSpec as P

C = 32
GY = 32
GX = 64
ZD = 4
A_DEV = 1536
TILES = 96
TILE_A = 64
TILE_C = 512
NB = 32
NAB = 24
CELLS = GY * GX
SLABS = 16
REPS = 8
W_CHUNKS = 6
W_STEP = TILES // W_CHUNKS

PREV_C, LAST_C = 0, 96
PREV_A, LAST_A = 128, 224
ATOM, CELL = 248, 344

F32 = jnp.float32
BF16 = jnp.bfloat16


def at(axis, index):
    return {axis: index}


def kernel(
    idx, feats, cot, w_hbm, conv, mix4, mix_t,
    pot, gfe, gout,
    w, src, acc, snd_dn, snd_up, rcv_lo, rcv_hi, shifted, dside, toep1, toep2, rep1, prod, gw,
    win, cacc, gp, rs1, piece, rs2, fin, ag,
    w_sem, h_send, h_recv, p_send, p_recv, s1, r1, s2, r2, s3, r3, s4, r4,
):
    slab = lax.axis_index("slab")
    rep = lax.axis_index("rep")
    up = lax.rem(slab + 1, SLABS)
    down = lax.rem(slab + SLABS - 1, SLABS)

    loads = []
    for k in range(W_CHUNKS):
        part = pl.ds(k * W_STEP, W_STEP)
        loads.append(pltpu.make_async_copy(w_hbm.at[part], w.at[part], w_sem.at[k]))
        loads[-1].start()

    barrier = pltpu.get_barrier_semaphore()
    for k in range(1, SLABS):
        pl.semaphore_signal(barrier, inc=1, device_id=at("slab", lax.rem(slab + k, SLABS)),
                            device_id_type=pl.DeviceIdType.MESH)
    for k in range(1, REPS):
        pl.semaphore_signal(barrier, inc=1, device_id=at("rep", lax.rem(rep + k, REPS)),
                            device_id_type=pl.DeviceIdType.MESH)

    for a in range(NAB):
        cols = slice(a * TILE_A, (a + 1) * TILE_A)
        src[a, :C] = feats[:, cols]
        src[a, C:] = cot[:, cols]
    acc[0] = jnp.zeros((2 * C, TILE_C), F32)
    cacc[0] = jnp.zeros((2 * C, TILE_A), F32)

    def deposit(t, carry):
        value = jnp.dot(src[idx[ATOM + t]], w[t], preferred_element_type=F32)
        acc[t + 1] = value + acc[idx[PREV_C + t]]
        return carry

    for k in range(W_CHUNKS):
        loads[k].wait()
        lax.fori_loop(k * W_STEP, (k + 1) * W_STEP, deposit, 0)

    for f in range(2):
        rows = slice(f * C, (f + 1) * C)
        for p in range(3):
            for q in range(4):
                snd_dn[f, p, q] = acc[idx[LAST_C + p * 4 + q], rows].astype(BF16)
                snd_up[f, p, q] = acc[idx[LAST_C + (p + 5) * 4 + q], rows].astype(BF16)

    pl.semaphore_wait(barrier, SLABS + REPS - 2)
    halos = []
    for f in range(2):
        for side, (source, target, to) in enumerate(((snd_dn, rcv_hi, down), (snd_up, rcv_lo, up))):
            halos.append(pltpu.make_async_remote_copy(
                src_ref=source.at[f], dst_ref=target.at[f],
                send_sem=h_send.at[f, side], recv_sem=h_recv.at[f, side],
                device_id=at("slab", to), device_id_type=pl.DeviceIdType.MESH))
            halos[-1].start()

    lane32 = lax.broadcasted_iota(jnp.int32, (C, 128), 1) // C

    def banded(toep, flip):
        for dx in range(3):
            for zo in range(4):
                for ct in range(5):
                    tile = jnp.zeros((C, 128), F32)
                    for g in range(4):
                        dy, zi = divmod(ct * 4 + g, 6)
                        if dy < 3 and 0 <= zi - zo < 3:
                            off = 9 * (zi - zo) + 3 * dy + dx
                            off = 26 - off if flip else off
                            tile = jnp.where(lane32 == g, rep1[pl.ds(off * C, C)], tile)
                    rows = slice((dx * 4 + zo) * C, (dx * 4 + zo + 1) * C)
                    width = 128 if ct < 4 else 64
                    toep[rows, ct * 128 : ct * 128 + width] = tile[:, :width].astype(BF16)

    rep1[...] = jnp.dot(conv[...], mix4[...], preferred_element_type=F32)
    banded(toep1, False)

    def turned(off, carry):
        part = conv[pl.ds(pl.multiple_of(off * C, C), C)]
        wide = jnp.concatenate([part] * 4, axis=0)
        rep1[pl.ds(pl.multiple_of(off * C, C), C)] = lax.dot_general(
            mix_t[...], wide, (((1,), (1,)), ((), ())), preferred_element_type=F32)
        return carry

    lax.fori_loop(0, 27, turned, 0)
    banded(toep2, True)

    lane = lax.broadcasted_iota(jnp.int32, (128, 128), 1)
    first_x = lax.rem(lane, GX) == 0
    last_x = lax.rem(lane, GX) == GX - 1

    def next_x(v):
        return jnp.where(last_x[: v.shape[0]], pltpu.roll(v, GX - 1, 1), pltpu.roll(v, 127, 1))

    def prev_x(v):
        return jnp.where(first_x[: v.shape[0]], pltpu.roll(v, 128 - GX + 1, 1), pltpu.roll(v, 1, 1))

    phis = []
    for f in range(2):
        rows = slice(f * C, (f + 1) * C)
        halos[2 * f].wait_recv()
        halos[2 * f + 1].wait_recv()
        for p in range(6):
            got = rcv_lo.at[f, p] if p < 3 else rcv_hi.at[f, p - 3]
            plane = jnp.concatenate(
                [acc[idx[LAST_C + (p + 1) * 4 + q], rows] + got[q].astype(F32) for q in range(4)], axis=1)
            own = slice(p * C, (p + 1) * C)
            shifted[f, 1, own] = plane.astype(BF16)
            shifted[f, 0, own] = pltpu.roll(plane, GX, 1).astype(BF16)
            shifted[f, 2, own] = pltpu.roll(plane, CELLS - GX, 1).astype(BF16)
        toep = toep2 if f else toep1
        for q in range(4):
            cols = slice(q * TILE_C, (q + 1) * TILE_C)
            stack = shifted[f, :, :, cols].reshape(18 * C, TILE_C)
            prod[...] = jnp.dot(toep[...], stack, preferred_element_type=F32)
            for h in range(4):
                part = slice(h * 128, (h + 1) * 128)
                low, mid, high = (prod[d * 128 : (d + 1) * 128, part] for d in range(3))
                phi = (mid + prev_x(low) + next_x(high)).astype(BF16)
                for z in range(ZD):
                    win[f, (z + 2) * 4 + q, :, part] = phi[z * C : (z + 1) * C]
        for side, (start, land, to) in enumerate(((8, 24, down), (16, 0, up))):
            phis.append(pltpu.make_async_remote_copy(
                src_ref=win.at[f, pl.ds(start, 8)], dst_ref=win.at[f, pl.ds(land, 8)],
                send_sem=p_send.at[f, side], recv_sem=p_recv.at[f, side],
                device_id=at("slab", to), device_id_type=pl.DeviceIdType.MESH))
            phis[-1].start()

    for k in range(16):
        cols = slice(k * 128, (k + 1) * 128)
        v = shifted[1, 1, C : 5 * C, cols].astype(F32)
        dside[:128, cols] = next_x(v).astype(BF16)
        dside[128:256, cols] = shifted[1, 1, C : 5 * C, cols]
        dside[256:, cols] = prev_x(v).astype(BF16)
    for dy in range(3):
        gw[dy] = lax.dot_general(dside[...], shifted[0, dy], (((1,), (1,)), ((), ())),
                                 preferred_element_type=F32)
    gp[...] = jnp.zeros_like(gp)
    for off in range(27):
        dz, dy, dx = off // 9, off // 3 % 3, off % 3
        total = None
        for zo in range(ZD):
            rows = slice((dx * 4 + zo) * C, (dx * 4 + zo + 1) * C)
            start = (zo + dz) * C
            part = gw[dy, rows, start : start + C]
            total = part if total is None else total + part
        gp[off // 4, :, off % 4 * C : (off % 4 + 1) * C] = total

    def send(source, target, s_sem, r_sem, axis, to):
        copy = pltpu.make_async_remote_copy(
            src_ref=source, dst_ref=target, send_sem=s_sem, recv_sem=r_sem,
            device_id=at(axis, to), device_id_type=pl.DeviceIdType.MESH)
        copy.start()
        return copy

    sent = []
    now = []
    for k in range(1, REPS):
        to = lax.rem(rep + k, REPS)
        now.append(send(gp.at[to], rs1.at[k], s1.at[k], r1.at[k], "rep", to))
    total = gp[rep]
    for k in range(1, REPS):
        now[k - 1].wait_recv()
        total = total + rs1[k]
    for s in range(SLABS):
        piece[s] = total[2 * s : 2 * s + 2]
    sent += now
    now = []
    for k in range(1, SLABS):
        to = lax.rem(slab + k, SLABS)
        now.append(send(piece.at[to], rs2.at[k], s2.at[k], r2.at[k], "slab", to))
    total = piece[slab]
    for k in range(1, SLABS):
        now[k - 1].wait_recv()
        total = total + rs2[k]
    fin[...] = total
    sent += now
    now = []
    for k in range(1, SLABS):
        to = lax.rem(slab + k, SLABS)
        now.append(send(fin, ag.at[slab], s3.at[k], r3.at[k], "slab", to))
    ag[slab] = fin[...]
    for copy in now:
        copy.wait_recv()
    sent += now
    now = []
    for k in range(1, REPS):
        to = lax.rem(rep + k, REPS)
        now.append(send(ag, gout.at[rep], s4.at[k], r4.at[k], "rep", to))
    gout[rep] = ag[...]

    for copy in phis:
        copy.wait_recv()

    def collect(t, carry):
        cell = idx[CELL + t]
        block = jnp.concatenate([win[0, cell], win[1, cell]], axis=0)
        value = lax.dot_general(block, w[t], (((1,), (1,)), ((), ())), preferred_element_type=F32)
        cacc[t + 1] = value + cacc[idx[PREV_A + t]]
        return carry

    lax.fori_loop(0, TILES, collect, 0)
    for a in range(0, NAB, 2):
        pair = jnp.concatenate([cacc[idx[LAST_A + a]], cacc[idx[LAST_A + a + 1]]], axis=1).astype(BF16)
        cols = slice(a * TILE_A, (a + 2) * TILE_A)
        pot[:, cols] = pair[:C]
        gfe[:, cols] = pair[C:]

    for copy in now:
        copy.wait_recv()
    for copy in sent + now + halos + phis:
        copy.wait_send()


def chains(cells, atoms, live):
    tiles = jnp.arange(TILES, dtype=jnp.int32)
    alive = (tiles < live)[None, :]
    before = tiles[None, :] < tiles[:, None]

    def newest(match):
        return jnp.max(jnp.where(match & alive, tiles[None, :] + 1, 0), axis=1)

    parts = []
    for ids, count in ((cells, NB), (atoms, NAB)):
        parts.append(newest((ids[None, :] == ids[:, None]) & before))
        parts.append(newest(ids[None, :] == jnp.arange(count, dtype=jnp.int32)[:, None]))
    return jnp.concatenate(parts + [atoms, cells])


def local(feats, tile_weight, tile_atom, tile_cell, tile_live, w_mix, conv_w, cotangent):
    idx = chains(tile_cell[0], tile_atom[0], tile_live[0, 0])
    vmem = pl.BlockSpec(memory_space=pltpu.VMEM)
    dma = pltpu.SemaphoreType.DMA
    pot, gfe, total = pl.pallas_call(
        kernel,
        out_shape=(
            jax.ShapeDtypeStruct((C, A_DEV), BF16),
            jax.ShapeDtypeStruct((C, A_DEV), BF16),
            jax.ShapeDtypeStruct((REPS, SLABS, 2, 128), F32),
        ),
        in_specs=[
            pl.BlockSpec(memory_space=pltpu.SMEM), vmem, vmem,
            pl.BlockSpec(memory_space=pl.ANY), vmem, vmem, vmem,
        ],
        out_specs=(vmem, vmem, vmem),
        scratch_shapes=[
            pltpu.VMEM((TILES, TILE_A, TILE_C), BF16),
            pltpu.VMEM((NAB, 2 * C, TILE_A), BF16),
            pltpu.VMEM((TILES + 1, 2 * C, TILE_C), F32),
            pltpu.VMEM((2, 3, 4, C, TILE_C), BF16),
            pltpu.VMEM((2, 3, 4, C, TILE_C), BF16),
            pltpu.VMEM((2, 3, 4, C, TILE_C), BF16),
            pltpu.VMEM((2, 3, 4, C, TILE_C), BF16),
            pltpu.VMEM((2, 3, 6 * C, CELLS), BF16),
            pltpu.VMEM((12 * C, CELLS), BF16),
            pltpu.VMEM((12 * C, 18 * C), BF16),
            pltpu.VMEM((12 * C, 18 * C), BF16),
            pltpu.VMEM((27 * C, 128), F32),
            pltpu.VMEM((12 * C, TILE_C), F32),
            pltpu.VMEM((3, 12 * C, 6 * C), F32),
            pltpu.VMEM((2, NB, C, TILE_C), BF16),
            pltpu.VMEM((TILES + 1, 2 * C, TILE_A), F32),
            pltpu.VMEM((REPS, C, 128), F32),
            pltpu.VMEM((REPS, C, 128), F32),
            pltpu.VMEM((SLABS, 2, 128), F32),
            pltpu.VMEM((SLABS, 2, 128), F32),
            pltpu.VMEM((2, 128), F32),
            pltpu.VMEM((SLABS, 2, 128), F32),
            dma((W_CHUNKS,)), dma((2, 2)), dma((2, 2)), dma((2, 2)), dma((2, 2)),
            dma((REPS,)), dma((REPS,)), dma((SLABS,)), dma((SLABS,)),
            dma((SLABS,)), dma((SLABS,)), dma((REPS,)), dma((REPS,)),
        ],
        compiler_params=pltpu.CompilerParams(
            collective_id=0, has_side_effects=True, vmem_limit_bytes=56 * 2**20,
        ),
    )(
        idx, feats[0], cotangent[0], tile_weight[0], conv_w.reshape(27 * C, C),
        jnp.tile(w_mix, (1, 4)), w_mix.T,
    )
    packed = total.reshape(REPS, C, 4, C)
    moments = jnp.transpose(packed, (0, 2, 1, 3)).reshape(REPS * 4, C, C)[:27]
    exact = lax.Precision.HIGHEST
    conv_total = jnp.einsum("koj,ij->koi", moments, w_mix.astype(F32), precision=exact)
    mix_total = jnp.einsum("kom,koi->mi", conv_w.astype(F32), moments, precision=exact)
    groups = REPS * SLABS
    conv_scale = math.sqrt(groups * ZD * GY * GX)
    mix_scale = math.sqrt(groups * A_DEV)
    return (pot[None], gfe[None], conv_total / conv_scale, mix_total / mix_scale)


def solution(mesh):
    return jax.shard_map(
        local,
        mesh=mesh,
        in_specs=(
            P("rep", None, "slab"),
            P("rep", "slab", None, None),
            P("rep", "slab"),
            P("rep", "slab"),
            P("rep", "slab"),
            P(),
            P(),
            P("rep", None, "slab"),
        ),
        out_specs=(P("rep", None, "slab"), P("rep", None, "slab"), P(), P()),
        check_vma=False,
    )
```

```python
import math

import jax
import jax.numpy as jnp
from jax import lax
from jax.experimental import pallas as pl
from jax.experimental.pallas import tpu as pltpu
from jax.sharding import PartitionSpec as P

C = 32
GY = 32
GX = 64
ZD = 4
A_DEV = 1536
TILES = 96
TILE_A = 64
TILE_C = 512
NB = 32
NAB = 24
CELLS = GY * GX
SLABS = 16
REPS = 8
W_CHUNKS = 6
W_STEP = TILES // W_CHUNKS

GROUP = 16
UNROLL = 8
PREV_C, LAST_C, PREV_A, LAST_A, ATOM, CELL = range(6)

F32 = jnp.float32
BF16 = jnp.bfloat16
NT = (((1,), (1,)), ((), ()))
MESH = pl.DeviceIdType.MESH


def kernel(
    feats_hbm, w_hbm, atom_hbm, cell_hbm, live, mix_hbm, conv_hbm, cot_hbm,
    pot, gfe, gout,
    feats, cot, conv, mix, atom_v, cell_v, idx_v, idx,
    w, src, acc, snd_dn, snd_up, rcv_lo, rcv_hi, shifted, dside, toep1, toep2, rep1, prod, gw,
    win, cacc, gp, rs1, rs2, piece, fin,
    in_sem, w_sem, h_send, h_recv, p_send, p_recv, g_send, g_recv,
):
    slab = lax.axis_index("slab")
    rep = lax.axis_index("rep")
    chip, core = slab // 2, lax.rem(slab, 2)
    up = lax.rem(slab + 1, SLABS)
    down = lax.rem(slab + SLABS - 1, SLABS)
    member = rep * 2 + core

    small = []
    pairs = ((cell_hbm, cell_v), (atom_hbm, atom_v), (feats_hbm, feats), (cot_hbm, cot),
             (mix_hbm, mix), (conv_hbm, conv))
    for k, (source, target) in enumerate(pairs):
        small.append(pltpu.make_async_copy(source, target, in_sem.at[k]))
        small[-1].start()
    loads = []
    for k in range(W_CHUNKS):
        part = pl.ds(k * W_STEP, W_STEP)
        loads.append(pltpu.make_async_copy(w_hbm.at[part], w.at[part], w_sem.at[k]))
        loads[-1].start()

    def plane_mate(k):
        other = lax.rem(member + k, GROUP)
        return {"rep": other // 2, "slab": chip * 2 + lax.rem(other, 2)}

    def row_mate(k):
        return {"slab": lax.rem(chip + k, SLABS // 2) * 2 + core}

    mates = [plane_mate(k) for k in range(1, GROUP)] + [row_mate(k) for k in range(1, SLABS // 2)]
    mates += [{"slab": up}, {"slab": down}]
    barrier = pltpu.get_barrier_semaphore()
    for mate in mates:
        pl.semaphore_signal(barrier, inc=1, device_id=mate, device_id_type=MESH)

    small[0].wait()
    small[1].wait()
    lane = lax.broadcasted_iota(jnp.int32, (TILES, TILES), 1)
    sub = lax.broadcasted_iota(jnp.int32, (TILES, TILES), 0)
    alive = sub < live[0, 0]
    number = sub + 1
    for ids, prev, last, copied, limit in (
        (cell_v, PREV_C, LAST_C, CELL, NB - 1), (atom_v, PREV_A, LAST_A, ATOM, NAB - 1)
    ):
        row = jnp.broadcast_to(ids[...], (TILES, TILES))
        column = jnp.sum(jnp.where(lane == sub, row, 0), axis=1, keepdims=True)
        before = jnp.where((column == row) & (sub < lane) & alive, number, 0)
        newest = jnp.where((column == lane) & alive, number, 0)
        idx_v[prev : prev + 1, :TILES] = jnp.clip(jnp.max(before, axis=0, keepdims=True), 0, TILES)
        idx_v[last : last + 1, :TILES] = jnp.clip(jnp.max(newest, axis=0, keepdims=True), 0, TILES)
        idx_v[copied : copied + 1, :TILES] = jnp.clip(ids[...], 0, limit)
    table = pltpu.make_async_copy(idx_v, idx, in_sem.at[6])
    table.start()

    small[2].wait()
    small[3].wait()
    for a in range(NAB):
        cols = slice(a * TILE_A, (a + 1) * TILE_A)
        src[a, :C] = feats[:, cols]
        src[a, C:] = cot[:, cols]
    acc[0] = jnp.zeros((2 * C, TILE_C), F32)
    cacc[0] = jnp.zeros((2 * C, TILE_A), F32)
    table.wait()

    def deposit(i, carry):
        first = i * UNROLL
        values = [jnp.dot(src[idx[ATOM, first + u]], w[first + u], preferred_element_type=F32) for u in range(UNROLL)]
        for u in range(UNROLL):
            acc[first + u + 1] = values[u] + acc[idx[PREV_C, first + u]]
        return carry

    steps = W_STEP // UNROLL
    for k in range(W_CHUNKS):
        loads[k].wait()
        lax.fori_loop(k * steps, (k + 1) * steps, deposit, 0)

    pl.semaphore_wait(barrier, len(mates))
    halos = []
    groups = []
    sides = ((snd_dn, rcv_hi, down, 0), (snd_up, rcv_lo, up, 5))
    for stage, (f, wanted) in enumerate(((0, ((0, 1, 2), (2, 1, 0))), (1, ((0, 1), (2, 1))), (1, ((2,), (0,))))):
        rows = slice(f * C, (f + 1) * C)
        for j in range(len(wanted[0])):
            for side, (source, target, to, base) in enumerate(sides):
                k = wanted[side][j]
                for q in range(4):
                    source[f, k, q] = acc[idx[LAST_C, (base + k) * 4 + q], rows].astype(BF16)
                copy = pltpu.make_async_remote_copy(
                    src_ref=source.at[f, k], dst_ref=target.at[f, k],
                    send_sem=h_send.at[stage, side], recv_sem=h_recv.at[stage, side],
                    device_id={"slab": to}, device_id_type=MESH)
                copy.start()
        for side, (source, target, to, base) in enumerate(sides):
            first, count = min(wanted[side]), len(wanted[side])
            halos.append(pltpu.make_async_remote_copy(
                src_ref=source.at[f, pl.ds(first, count)], dst_ref=target.at[f, pl.ds(first, count)],
                send_sem=h_send.at[stage, side], recv_sem=h_recv.at[stage, side],
                device_id={"slab": to}, device_id_type=MESH))

    small[4].wait()
    small[5].wait()
    lane32 = lax.broadcasted_iota(jnp.int32, (C, 128), 1) // C

    def banded(toep, flip):
        for dx in range(3):
            for zo in range(4):
                for ct in range(5):
                    tile = jnp.zeros((C, 128), F32)
                    for g in range(4):
                        dy, zi = divmod(ct * 4 + g, 6)
                        if dy < 3 and 0 <= zi - zo < 3:
                            off = 9 * (zi - zo) + 3 * dy + dx
                            off = 26 - off if flip else off
                            tile = jnp.where(lane32 == g, rep1[pl.ds(off * C, C)], tile)
                    rows = slice((dx * 4 + zo) * C, (dx * 4 + zo + 1) * C)
                    width = 128 if ct < 4 else 64
                    toep[rows, ct * 128 : ct * 128 + width] = tile[:, :width].astype(BF16)

    mixing = mix[...]
    rep1[...] = jnp.dot(
        conv[...].reshape(27 * C, C), jnp.concatenate([mixing] * 4, axis=1), preferred_element_type=F32)
    banded(toep1, False)
    mix_t = mixing.astype(F32).T.astype(BF16)

    def turned(off, carry):
        wide = jnp.concatenate([conv[off]] * 4, axis=0)
        rep1[pl.ds(pl.multiple_of(off * C, C), C)] = lax.dot_general(mix_t, wide, NT, preferred_element_type=F32)
        return carry

    lax.fori_loop(0, 27, turned, 0)
    banded(toep2, True)

    spot = lax.broadcasted_iota(jnp.int32, (128, 128), 1)
    first_x = lax.rem(spot, GX) == 0
    last_x = lax.rem(spot, GX) == GX - 1

    def next_x(v):
        return jnp.where(last_x, pltpu.roll(v, GX - 1, 1), pltpu.roll(v, 127, 1))

    def prev_x(v):
        return jnp.where(first_x, pltpu.roll(v, 128 - GX + 1, 1), pltpu.roll(v, 1, 1))

    def stack(f, p):
        got = rcv_lo.at[f, p] if p < 3 else rcv_hi.at[f, p - 3]
        rows = slice(f * C, (f + 1) * C)
        plane = jnp.concatenate(
            [acc[idx[LAST_C, (p + 1) * 4 + q], rows] + got[q].astype(F32) for q in range(4)], axis=1)
        own = slice(p * C, (p + 1) * C)
        shifted[f, 1, own] = plane.astype(BF16)
        shifted[f, 0, own] = pltpu.roll(plane, GX, 1).astype(BF16)
        shifted[f, 2, own] = pltpu.roll(plane, CELLS - GX, 1).astype(BF16)

    phis = []

    def convolve(f):
        toep = toep2 if f else toep1
        for q in range(4):
            cols = slice(q * TILE_C, (q + 1) * TILE_C)
            stacked = shifted[f, :, :, cols].reshape(18 * C, TILE_C)
            prod[...] = jnp.dot(toep[...], stacked, preferred_element_type=F32)
            for h in range(4):
                part = slice(h * 128, (h + 1) * 128)
                low, mid, high = (prod[d * 128 : (d + 1) * 128, part] for d in range(3))
                phi = (mid + prev_x(low) + next_x(high)).astype(BF16)
                for z in range(ZD):
                    win[f, (z + 2) * 4 + q, :, part] = phi[z * C : (z + 1) * C]
        for side, (start, land, to) in enumerate(((8, 24, down), (16, 0, up))):
            phis.append(pltpu.make_async_remote_copy(
                src_ref=win.at[f, pl.ds(start, 8)], dst_ref=win.at[f, pl.ds(land, 8)],
                send_sem=p_send.at[f, side], recv_sem=p_recv.at[f, side],
                device_id={"slab": to}, device_id_type=MESH))
            phis[-1].start()

    halos[0].wait_recv()
    halos[1].wait_recv()
    for p in range(6):
        stack(0, p)
    convolve(0)

    halos[2].wait_recv()
    halos[3].wait_recv()
    for p in range(1, 5):
        stack(1, p)
    for k in range(16):
        cols = slice(k * 128, (k + 1) * 128)
        v = shifted[1, 1, C : 5 * C, cols].astype(F32)
        dside[:128, cols] = next_x(v).astype(BF16)
        dside[128:256, cols] = shifted[1, 1, C : 5 * C, cols]
        dside[256:, cols] = prev_x(v).astype(BF16)
    for dy in range(3):
        gw[dy] = lax.dot_general(dside[...], shifted[0, dy], NT, preferred_element_type=F32)
    for off in range(27):
        dz, dy, dx = off // 9, off // 3 % 3, off % 3
        total = None
        for zo in range(ZD):
            rows = slice((dx * 4 + zo) * C, (dx * 4 + zo + 1) * C)
            start = (zo + dz) * C
            part = gw[dy, rows, start : start + C]
            total = part if total is None else total + part
        block, cols = off // 4, slice(off % 4 * C, (off % 4 + 1) * C)
        gp[2 * block, :, cols] = total[: C // 2]
        gp[2 * block + 1, :, cols] = total[C // 2 :]
    gp[13, :, 3 * C :] = jnp.zeros((C // 2, C), F32)
    gp[12, :, 3 * C :] = jnp.zeros((C // 2, C), F32)
    gp[14:] = jnp.zeros((2, C // 2, 128), F32)

    def give(source, target, phase, mate):
        pltpu.make_async_remote_copy(
            src_ref=source, dst_ref=target, send_sem=g_send.at[phase], recv_sem=g_recv.at[phase],
            device_id=mate, device_id_type=MESH).start()

    def all_of(buffer, count, phase):
        part = buffer.at[pl.ds(0, count)]
        return pltpu.make_async_remote_copy(
            src_ref=part, dst_ref=part, send_sem=g_send.at[phase], recv_sem=g_recv.at[phase],
            device_id=plane_mate(1), device_id_type=MESH)

    for k in range(1, GROUP):
        give(gp.at[lax.rem(member + k, GROUP)], rs1.at[k], 0, plane_mate(k))
    rs1[0] = gp[member]

    halos[4].wait_recv()
    halos[5].wait_recv()
    stack(1, 0)
    stack(1, 5)
    convolve(1)

    all_of(rs1, GROUP - 1, 0).wait_recv()
    piece[...] = jnp.sum(rs1[...], axis=0)
    for k in range(1, SLABS // 2):
        give(piece, rs2.at[chip], 1, row_mate(k))
    rs2[chip] = piece[...]

    for copy in phis:
        copy.wait_recv()

    def collect(i, carry):
        first = i * UNROLL
        values = []
        for u in range(UNROLL):
            cell = idx[CELL, first + u]
            block = jnp.concatenate([win[0, cell], win[1, cell]], axis=0)
            values.append(lax.dot_general(block, w[first + u], NT, preferred_element_type=F32))
        for u in range(UNROLL):
            cacc[first + u + 1] = values[u] + cacc[idx[PREV_A, first + u]]
        return carry

    lax.fori_loop(0, 4, collect, 0)

    all_of(rs2, SLABS // 2 - 1, 1).wait_recv()
    fin[...] = jnp.sum(rs2[...], axis=0)
    for k in range(1, GROUP):
        give(fin, gout.at[member], 2, plane_mate(k))
    gout[member] = fin[...]

    lax.fori_loop(4, TILES // UNROLL, collect, 0)
    for a in range(0, NAB, 2):
        pair = jnp.concatenate([cacc[idx[LAST_A, a]], cacc[idx[LAST_A, a + 1]]], axis=1).astype(BF16)
        cols = slice(a * TILE_A, (a + 2) * TILE_A)
        pot[:, cols] = pair[:C]
        gfe[:, cols] = pair[C:]

    all_of(gout, GROUP - 1, 2).wait_recv()
    all_of(gout, GROUP - 1, 2).wait_send()
    all_of(rs2, SLABS // 2 - 1, 1).wait_send()
    all_of(rs1, GROUP - 1, 0).wait_send()
    for copy in halos + phis:
        copy.wait_send()


def finish(pot_in, gfe_in, moments, mix, conv, pot, gfe, gconv, gmix, flat):
    pot[...] = pot_in[...]
    gfe[...] = gfe_in[...]
    for off in range(27):
        block, cols = off // 4, slice(off % 4 * C, (off % 4 + 1) * C)
        flat[off * C : off * C + C // 2] = moments[2 * block, :, cols]
        flat[off * C + C // 2 : (off + 1) * C] = moments[2 * block + 1, :, cols]
    value = flat[...]
    high = value.astype(BF16)
    low = (value - high.astype(F32)).astype(BF16)
    mixing = mix[...]
    turned = conv[...].reshape(27 * C, C).astype(F32).T.astype(BF16)
    devices = REPS * SLABS
    conv_scale = 1.0 / math.sqrt(devices * ZD * GY * GX)
    mix_scale = 1.0 / math.sqrt(devices * A_DEV)
    product = (lax.dot_general(high, mixing, NT, preferred_element_type=F32)
               + lax.dot_general(low, mixing, NT, preferred_element_type=F32))
    gconv[...] = (product * conv_scale).reshape(27, C, C)
    gmix[...] = (jnp.dot(turned, high, preferred_element_type=F32)
                 + jnp.dot(turned, low, preferred_element_type=F32)) * mix_scale


def local(feats, tile_weight, tile_atom, tile_cell, tile_live, w_mix, conv_w, cotangent):
    vmem = pl.BlockSpec(memory_space=pltpu.VMEM)
    hbm = pl.BlockSpec(memory_space=pl.ANY)
    dma = pltpu.SemaphoreType.DMA
    field = jax.ShapeDtypeStruct((C, A_DEV), BF16)
    pot, gfe, total = pl.pallas_call(
        kernel,
        out_shape=(field, field, jax.ShapeDtypeStruct((GROUP, C // 2, 128), F32)),
        in_specs=[hbm] * 4 + [pl.BlockSpec(memory_space=pltpu.SMEM)] + [hbm] * 3,
        out_specs=(vmem, vmem, vmem),
        scratch_shapes=[
            pltpu.VMEM((C, A_DEV), BF16),
            pltpu.VMEM((C, A_DEV), BF16),
            pltpu.VMEM((27, C, C), BF16),
            pltpu.VMEM((C, C), BF16),
            pltpu.VMEM((1, TILES), jnp.int32),
            pltpu.VMEM((1, TILES), jnp.int32),
            pltpu.VMEM((8, 128), jnp.int32),
            pltpu.SMEM((8, 128), jnp.int32),
            pltpu.VMEM((TILES, TILE_A, TILE_C), BF16),
            pltpu.VMEM((NAB, 2 * C, TILE_A), BF16),
            pltpu.VMEM((TILES + 1, 2 * C, TILE_C), F32),
            pltpu.VMEM((2, 3, 4, C, TILE_C), BF16),
            pltpu.VMEM((2, 3, 4, C, TILE_C), BF16),
            pltpu.VMEM((2, 3, 4, C, TILE_C), BF16),
            pltpu.VMEM((2, 3, 4, C, TILE_C), BF16),
            pltpu.VMEM((2, 3, 6 * C, CELLS), BF16),
            pltpu.VMEM((12 * C, CELLS), BF16),
            pltpu.VMEM((12 * C, 18 * C), BF16),
            pltpu.VMEM((12 * C, 18 * C), BF16),
            pltpu.VMEM((27 * C, 128), F32),
            pltpu.VMEM((12 * C, TILE_C), F32),
            pltpu.VMEM((3, 12 * C, 6 * C), F32),
            pltpu.VMEM((2, NB, C, TILE_C), BF16),
            pltpu.VMEM((TILES + 1, 2 * C, TILE_A), F32),
            pltpu.VMEM((GROUP, C // 2, 128), F32),
            pltpu.VMEM((GROUP, C // 2, 128), F32),
            pltpu.VMEM((SLABS // 2, C // 2, 128), F32),
            pltpu.VMEM((C // 2, 128), F32),
            pltpu.VMEM((C // 2, 128), F32),
            dma((7,)), dma((W_CHUNKS,)), dma((3, 2)), dma((3, 2)), dma((2, 2)), dma((2, 2)), dma((3,)), dma((3,)),
        ],
        compiler_params=pltpu.CompilerParams(
            collective_id=0, has_side_effects=True, vmem_limit_bytes=56 * 2**20,
        ),
    )(feats[0], tile_weight[0], tile_atom, tile_cell, tile_live, w_mix, conv_w, cotangent[0])
    pot, gfe, gconv, gmix = pl.pallas_call(
        finish,
        out_shape=(field, field, jax.ShapeDtypeStruct((27, C, C), F32), jax.ShapeDtypeStruct((C, C), F32)),
        in_specs=[vmem] * 5,
        out_specs=(vmem,) * 4,
        scratch_shapes=[pltpu.VMEM((27 * C, C), F32)],
        compiler_params=pltpu.CompilerParams(vmem_limit_bytes=32 * 2**20),
    )(pot, gfe, total, w_mix, conv_w)
    return pot[None], gfe[None], gconv, gmix


def solution(mesh):
    return jax.shard_map(
        local,
        mesh=mesh,
        in_specs=(
            P("rep", None, "slab"),
            P("rep", "slab", None, None),
            P("rep", "slab"),
            P("rep", "slab"),
            P("rep", "slab"),
            P(),
            P(),
            P("rep", None, "slab"),
        ),
        out_specs=(P("rep", None, "slab"), P("rep", None, "slab"), P(), P()),
        check_vma=False,
    )
```

```python
import math

import jax
import jax.numpy as jnp
from jax import lax
from jax.experimental import pallas as pl
from jax.experimental.pallas import tpu as pltpu
from jax.sharding import PartitionSpec as P

C = 32
GY = 32
GX = 64
ZD = 4
A_DEV = 1536
TILES = 96
TILE_A = 64
TILE_C = 512
NB = 32
NAB = 24
CELLS = GY * GX
SLABS = 16
REPS = 8
W_CHUNKS = 6
W_STEP = TILES // W_CHUNKS

GROUP = 16
UNROLL = 8
PREV_C, LAST_C, PREV_A, LAST_A, ATOM, CELL = range(6)

F32 = jnp.float32
BF16 = jnp.bfloat16
NT = (((1,), (1,)), ((), ()))
MESH = pl.DeviceIdType.MESH


def kernel(
    feats_hbm, w_hbm, atom_hbm, cell_hbm, live, mix_hbm, conv_hbm, cot_hbm,
    pot, gfe, gout,
    pot_v, gfe_v, feats, cot, conv, mix, atom_v, cell_v, idx_v, idx,
    w, src, acc, snd_dn, snd_up, rcv_lo, rcv_hi, shifted, dside, toep1, toep2, rep1, prod, gw,
    win0, win1, cacc, gp, rs1, rs2, piece, fin,
    in_sem, out_sem, w_sem, h_send, h_recv, p_send, p_recv, g_send, g_recv,
):
    slab = lax.axis_index("slab")
    rep = lax.axis_index("rep")
    chip, core = slab // 2, lax.rem(slab, 2)
    up = lax.rem(slab + 1, SLABS)
    down = lax.rem(slab + SLABS - 1, SLABS)
    member = rep * 2 + core

    small = []
    pairs = ((cell_hbm, cell_v), (atom_hbm, atom_v), (feats_hbm, feats), (mix_hbm, mix),
             (conv_hbm, conv), (cot_hbm, cot))
    for k, (source, target) in enumerate(pairs):
        small.append(pltpu.make_async_copy(source, target, in_sem.at[k]))
        small[-1].start()
    loads = []
    for k in range(W_CHUNKS):
        part = pl.ds(k * W_STEP, W_STEP)
        loads.append(pltpu.make_async_copy(w_hbm.at[part], w.at[part], w_sem.at[k]))
        loads[-1].start()

    def plane_mate(k):
        other = lax.rem(member + k, GROUP)
        return {"rep": other // 2, "slab": chip * 2 + lax.rem(other, 2)}

    def row_mate(k):
        return {"slab": lax.rem(chip + k, SLABS // 2) * 2 + core}

    mates = [plane_mate(k) for k in range(1, GROUP)] + [row_mate(k) for k in range(1, SLABS // 2)]
    mates += [{"slab": up}, {"slab": down}]
    barrier = pltpu.get_barrier_semaphore()
    for mate in mates:
        pl.semaphore_signal(barrier, inc=1, device_id=mate, device_id_type=MESH)

    small[0].wait()
    small[1].wait()
    lane = lax.broadcasted_iota(jnp.int32, (TILES, TILES), 1)
    sub = lax.broadcasted_iota(jnp.int32, (TILES, TILES), 0)
    alive = sub < live[0, 0]
    number = sub + 1
    for ids, prev, last, copied, limit in (
        (cell_v, PREV_C, LAST_C, CELL, NB - 1), (atom_v, PREV_A, LAST_A, ATOM, NAB - 1)
    ):
        row = jnp.broadcast_to(ids[...], (TILES, TILES))
        column = jnp.sum(jnp.where(lane == sub, row, 0), axis=1, keepdims=True)
        before = jnp.where((column == row) & (sub < lane) & alive, number, 0)
        newest = jnp.where((column == lane) & alive, number, 0)
        idx_v[prev : prev + 1, :TILES] = jnp.clip(jnp.max(before, axis=0, keepdims=True), 0, TILES)
        idx_v[last : last + 1, :TILES] = jnp.clip(jnp.max(newest, axis=0, keepdims=True), 0, TILES)
        idx_v[copied : copied + 1, :TILES] = jnp.clip(ids[...], 0, limit)
    table = pltpu.make_async_copy(idx_v, idx, in_sem.at[6])
    table.start()

    def fill(f, values):
        for a in range(NAB):
            src[f, a] = values[:, a * TILE_A : (a + 1) * TILE_A]
        acc[f, 0] = jnp.zeros((C, TILE_C), F32)
        cacc[f, 0] = jnp.zeros((C, TILE_A), F32)

    small[2].wait()
    fill(0, feats)
    table.wait()

    def deposit(f, start, stop):
        def body(i, carry):
            first = i * UNROLL
            values = [jnp.dot(src[f, idx[ATOM, first + u]], w[first + u], preferred_element_type=F32)
                      for u in range(UNROLL)]
            for u in range(UNROLL):
                acc[f, first + u + 1] = values[u] + acc[f, idx[PREV_C, first + u]]
            return carry

        lax.fori_loop(start // UNROLL, stop // UNROLL, body, 0)

    for k in range(W_CHUNKS):
        loads[k].wait()
        deposit(0, k * W_STEP, (k + 1) * W_STEP)

    halos = []
    sides = ((snd_dn, rcv_hi, down, 0), (snd_up, rcv_lo, up, 5))

    def exchange(stage, f, wanted):
        for j in range(len(wanted[0])):
            for side, (source, target, to, base) in enumerate(sides):
                k = wanted[side][j]
                for q in range(4):
                    source[f, k, q] = acc[f, idx[LAST_C, (base + k) * 4 + q]].astype(BF16)
                copy = pltpu.make_async_remote_copy(
                    src_ref=source.at[f, k], dst_ref=target.at[f, k],
                    send_sem=h_send.at[stage, side], recv_sem=h_recv.at[stage, side],
                    device_id={"slab": to}, device_id_type=MESH)
                copy.start()
        for side, (source, target, to, base) in enumerate(sides):
            first, count = min(wanted[side]), len(wanted[side])
            halos.append(pltpu.make_async_remote_copy(
                src_ref=source.at[f, pl.ds(first, count)], dst_ref=target.at[f, pl.ds(first, count)],
                send_sem=h_send.at[stage, side], recv_sem=h_recv.at[stage, side],
                device_id={"slab": to}, device_id_type=MESH))

    pl.semaphore_wait(barrier, len(mates))
    exchange(0, 0, ((0, 1, 2), (2, 1, 0)))
    small[5].wait()
    fill(1, cot)
    deposit(1, 0, TILES)
    exchange(1, 1, ((0, 1), (2, 1)))
    exchange(2, 1, ((2,), (0,)))

    small[3].wait()
    small[4].wait()
    lane32 = lax.broadcasted_iota(jnp.int32, (C, 128), 1) // C

    def banded(toep, flip):
        for dx in range(3):
            for zo in range(4):
                for ct in range(5):
                    tile = jnp.zeros((C, 128), F32)
                    for g in range(4):
                        dy, zi = divmod(ct * 4 + g, 6)
                        if dy < 3 and 0 <= zi - zo < 3:
                            off = 9 * (zi - zo) + 3 * dy + dx
                            off = 26 - off if flip else off
                            tile = jnp.where(lane32 == g, rep1[pl.ds(off * C, C)], tile)
                    rows = slice((dx * 4 + zo) * C, (dx * 4 + zo + 1) * C)
                    width = 128 if ct < 4 else 64
                    toep[rows, ct * 128 : ct * 128 + width] = tile[:, :width].astype(BF16)

    mixing = mix[...]
    rep1[...] = jnp.dot(
        conv[...].reshape(27 * C, C), jnp.concatenate([mixing] * 4, axis=1), preferred_element_type=F32)
    banded(toep1, False)
    mix_t = mixing.astype(F32).T.astype(BF16)

    for off in range(27):
        wide = jnp.concatenate([conv[off]] * 4, axis=0)
        rep1[off * C : (off + 1) * C] = lax.dot_general(mix_t, wide, NT, preferred_element_type=F32)
    banded(toep2, True)

    spot = lax.broadcasted_iota(jnp.int32, (128, 128), 1)
    first_x = lax.rem(spot, GX) == 0
    last_x = lax.rem(spot, GX) == GX - 1

    def next_x(v):
        return jnp.where(last_x, pltpu.roll(v, GX - 1, 1), pltpu.roll(v, 127, 1))

    def prev_x(v):
        return jnp.where(first_x, pltpu.roll(v, 128 - GX + 1, 1), pltpu.roll(v, 1, 1))

    def stack(f, p):
        got = rcv_lo.at[f, p] if p < 3 else rcv_hi.at[f, p - 3]
        plane = jnp.concatenate(
            [acc[f, idx[LAST_C, (p + 1) * 4 + q]] + got[q].astype(F32) for q in range(4)], axis=1)
        own = slice(p * C, (p + 1) * C)
        shifted[f, 1, own] = plane.astype(BF16)
        shifted[f, 0, own] = pltpu.roll(plane, GX, 1).astype(BF16)
        shifted[f, 2, own] = pltpu.roll(plane, CELLS - GX, 1).astype(BF16)

    phis = []
    win = (win0, win1)

    def convolve(f):
        toep = toep2 if f else toep1
        for q in range(4):
            cols = slice(q * TILE_C, (q + 1) * TILE_C)
            stacked = shifted[f, :, :, cols].reshape(18 * C, TILE_C)
            prod[...] = jnp.dot(toep[...], stacked, preferred_element_type=F32)
            for h in range(4):
                part = slice(h * 128, (h + 1) * 128)
                low, mid, high = (prod[d * 128 : (d + 1) * 128, part] for d in range(3))
                phi = (mid + prev_x(low) + next_x(high)).astype(BF16)
                for z in range(ZD):
                    win[f][(z + 2) * 4 + q, :, part] = phi[z * C : (z + 1) * C]
        for side, (start, land, to) in enumerate(((8, 24, down), (16, 0, up))):
            phis.append(pltpu.make_async_remote_copy(
                src_ref=win[f].at[pl.ds(start, 8)], dst_ref=win[f].at[pl.ds(land, 8)],
                send_sem=p_send.at[f, side], recv_sem=p_recv.at[f, side],
                device_id={"slab": to}, device_id_type=MESH))
            phis[-1].start()

    halos[0].wait_recv()
    halos[1].wait_recv()
    for p in range(6):
        stack(0, p)
    convolve(0)

    halos[2].wait_recv()
    halos[3].wait_recv()
    for p in range(1, 5):
        stack(1, p)
    for k in range(16):
        cols = slice(k * 128, (k + 1) * 128)
        v = shifted[1, 1, C : 5 * C, cols].astype(F32)
        dside[:128, cols] = next_x(v).astype(BF16)
        dside[128:256, cols] = shifted[1, 1, C : 5 * C, cols]
        dside[256:, cols] = prev_x(v).astype(BF16)
    for dy in range(3):
        gw[dy] = lax.dot_general(dside[...], shifted[0, dy], NT, preferred_element_type=F32)
    for off in range(27):
        dz, dy, dx = off // 9, off // 3 % 3, off % 3
        total = None
        for zo in range(ZD):
            rows = slice((dx * 4 + zo) * C, (dx * 4 + zo + 1) * C)
            start = (zo + dz) * C
            part = gw[dy, rows, start : start + C]
            total = part if total is None else total + part
        block, cols = off // 4, slice(off % 4 * C, (off % 4 + 1) * C)
        gp[2 * block, :, cols] = total[: C // 2]
        gp[2 * block + 1, :, cols] = total[C // 2 :]
    gp[13, :, 3 * C :] = jnp.zeros((C // 2, C), F32)
    gp[12, :, 3 * C :] = jnp.zeros((C // 2, C), F32)
    gp[14:] = jnp.zeros((2, C // 2, 128), F32)

    def give(source, target, phase, mate):
        pltpu.make_async_remote_copy(
            src_ref=source, dst_ref=target, send_sem=g_send.at[phase], recv_sem=g_recv.at[phase],
            device_id=mate, device_id_type=MESH).start()

    def all_of(buffer, count, phase):
        part = buffer.at[pl.ds(0, count)]
        return pltpu.make_async_remote_copy(
            src_ref=part, dst_ref=part, send_sem=g_send.at[phase], recv_sem=g_recv.at[phase],
            device_id=plane_mate(1), device_id_type=MESH)

    for k in range(1, GROUP):
        give(gp.at[lax.rem(member + k, GROUP)], rs1.at[k], 0, plane_mate(k))
    rs1[0] = gp[member]

    halos[4].wait_recv()
    halos[5].wait_recv()
    stack(1, 0)
    stack(1, 5)
    convolve(1)

    all_of(rs1, GROUP - 1, 0).wait_recv()
    piece[...] = jnp.sum(rs1[...], axis=0)
    for k in range(1, SLABS // 2):
        give(piece, rs2.at[chip], 1, row_mate(k))
    rs2[chip] = piece[...]

    def collect(f):
        def body(i, carry):
            first = i * UNROLL
            values = [lax.dot_general(win[f][idx[CELL, first + u]], w[first + u], NT, preferred_element_type=F32)
                      for u in range(UNROLL)]
            for u in range(UNROLL):
                cacc[f, first + u + 1] = values[u] + cacc[f, idx[PREV_A, first + u]]
            return carry

        lax.fori_loop(0, TILES // UNROLL, body, 0)
        out_v, out = (gfe_v, gfe) if f else (pot_v, pot)
        for a in range(0, NAB, 2):
            pair = jnp.concatenate([cacc[f, idx[LAST_A, a]], cacc[f, idx[LAST_A, a + 1]]], axis=1)
            out_v[:, a * TILE_A : (a + 2) * TILE_A] = pair.astype(BF16)
        copy = pltpu.make_async_copy(out_v, out, out_sem.at[f])
        copy.start()
        return copy

    phis[0].wait_recv()
    phis[1].wait_recv()
    outs = [collect(0)]

    all_of(rs2, SLABS // 2 - 1, 1).wait_recv()
    fin[...] = jnp.sum(rs2[...], axis=0)
    for k in range(1, GROUP):
        give(fin, gout.at[member], 2, plane_mate(k))
    outs.append(pltpu.make_async_copy(fin, gout.at[member], out_sem.at[2]))
    outs[-1].start()

    phis[2].wait_recv()
    phis[3].wait_recv()
    outs.append(collect(1))

    all_of(rs1, GROUP - 1, 0).wait_send()
    all_of(rs2, SLABS // 2 - 1, 1).wait_send()
    for copy in halos + phis:
        copy.wait_send()
    all_of(rs1, GROUP - 1, 2).wait_send()
    all_of(rs1, GROUP - 1, 2).wait_recv()
    for copy in outs:
        copy.wait()


def finish(pot_in, gfe_in, moments_hbm, mix_hbm, conv_hbm, pot, gfe, gconv, gmix, moments, mix, conv, flat, sem):
    pairs = ((moments_hbm, moments), (mix_hbm, mix), (conv_hbm, conv), (pot_in, pot), (gfe_in, gfe))
    copies = [pltpu.make_async_copy(source, target, sem.at[k]) for k, (source, target) in enumerate(pairs)]
    for copy in copies:
        copy.start()
    for copy in copies[:3]:
        copy.wait()
    for off in range(27):
        block, cols = off // 4, slice(off % 4 * C, (off % 4 + 1) * C)
        flat[off * C : off * C + C // 2] = moments[2 * block, :, cols]
        flat[off * C + C // 2 : (off + 1) * C] = moments[2 * block + 1, :, cols]
    value = flat[...]
    high = value.astype(BF16)
    low = (value - high.astype(F32)).astype(BF16)
    mixing = mix[...]
    turned = conv[...].reshape(27 * C, C).astype(F32).T.astype(BF16)
    devices = REPS * SLABS
    conv_scale = 1.0 / math.sqrt(devices * ZD * GY * GX)
    mix_scale = 1.0 / math.sqrt(devices * A_DEV)
    product = (lax.dot_general(high, mixing, NT, preferred_element_type=F32)
               + lax.dot_general(low, mixing, NT, preferred_element_type=F32))
    gconv[...] = (product * conv_scale).reshape(27, C, C)
    gmix[...] = (jnp.dot(turned, high, preferred_element_type=F32)
                 + jnp.dot(turned, low, preferred_element_type=F32)) * mix_scale
    for copy in copies[3:]:
        copy.wait()


def local(feats, tile_weight, tile_atom, tile_cell, tile_live, w_mix, conv_w, cotangent):
    vmem = pl.BlockSpec(memory_space=pltpu.VMEM)
    hbm = pl.BlockSpec(memory_space=pltpu.HBM)
    dma = pltpu.SemaphoreType.DMA
    field = jax.ShapeDtypeStruct((C, A_DEV), BF16)
    pot, gfe, total = pl.pallas_call(
        kernel,
        out_shape=(field, field, jax.ShapeDtypeStruct((GROUP, C // 2, 128), F32)),
        in_specs=[hbm] * 4 + [pl.BlockSpec(memory_space=pltpu.SMEM)] + [hbm] * 3,
        out_specs=(hbm, hbm, hbm),
        scratch_shapes=[
            pltpu.VMEM((C, A_DEV), BF16),
            pltpu.VMEM((C, A_DEV), BF16),
            pltpu.VMEM((C, A_DEV), BF16),
            pltpu.VMEM((C, A_DEV), BF16),
            pltpu.VMEM((27, C, C), BF16),
            pltpu.VMEM((C, C), BF16),
            pltpu.VMEM((1, TILES), jnp.int32),
            pltpu.VMEM((1, TILES), jnp.int32),
            pltpu.VMEM((8, 128), jnp.int32),
            pltpu.SMEM((8, 128), jnp.int32),
            pltpu.VMEM((TILES, TILE_A, TILE_C), BF16),
            pltpu.VMEM((2, NAB, C, TILE_A), BF16),
            pltpu.VMEM((2, TILES + 1, C, TILE_C), F32),
            pltpu.VMEM((2, 3, 4, C, TILE_C), BF16),
            pltpu.VMEM((2, 3, 4, C, TILE_C), BF16),
            pltpu.VMEM((2, 3, 4, C, TILE_C), BF16),
            pltpu.VMEM((2, 3, 4, C, TILE_C), BF16),
            pltpu.VMEM((2, 3, 6 * C, CELLS), BF16),
            pltpu.VMEM((12 * C, CELLS), BF16),
            pltpu.VMEM((12 * C, 18 * C), BF16),
            pltpu.VMEM((12 * C, 18 * C), BF16),
            pltpu.VMEM((27 * C, 128), F32),
            pltpu.VMEM((12 * C, TILE_C), F32),
            pltpu.VMEM((3, 12 * C, 6 * C), F32),
            pltpu.VMEM((NB, C, TILE_C), BF16),
            pltpu.VMEM((NB, C, TILE_C), BF16),
            pltpu.VMEM((2, TILES + 1, C, TILE_A), F32),
            pltpu.VMEM((GROUP, C // 2, 128), F32),
            pltpu.VMEM((GROUP, C // 2, 128), F32),
            pltpu.VMEM((SLABS // 2, C // 2, 128), F32),
            pltpu.VMEM((C // 2, 128), F32),
            pltpu.VMEM((C // 2, 128), F32),
            dma((7,)), dma((3,)), dma((W_CHUNKS,)), dma((3, 2)), dma((3, 2)), dma((2, 2)), dma((2, 2)), dma((3,)), dma((3,)),
        ],
        compiler_params=pltpu.CompilerParams(
            collective_id=0, has_side_effects=True, vmem_limit_bytes=56 * 2**20,
        ),
    )(feats[0], tile_weight[0], tile_atom, tile_cell, tile_live, w_mix, conv_w, cotangent[0])
    pot, gfe, gconv, gmix = pl.pallas_call(
        finish,
        out_shape=(field, field, jax.ShapeDtypeStruct((27, C, C), F32), jax.ShapeDtypeStruct((C, C), F32)),
        in_specs=[hbm] * 5,
        out_specs=(vmem,) * 4,
        scratch_shapes=[
            pltpu.VMEM((GROUP, C // 2, 128), F32),
            pltpu.VMEM((C, C), BF16),
            pltpu.VMEM((27, C, C), BF16),
            pltpu.VMEM((27 * C, C), F32),
            dma((5,)),
        ],
    )(pot, gfe, total, w_mix, conv_w)
    return pot[None], gfe[None], gconv, gmix


def solution(mesh):
    return jax.shard_map(
        local,
        mesh=mesh,
        in_specs=(
            P("rep", None, "slab"),
            P("rep", "slab", None, None),
            P("rep", "slab"),
            P("rep", "slab"),
            P("rep", "slab"),
            P(),
            P(),
            P("rep", None, "slab"),
        ),
        out_specs=(P("rep", None, "slab"), P("rep", None, "slab"), P(), P()),
        check_vma=False,
    )
```

```python
import math

import jax
import jax.numpy as jnp
from jax import lax
from jax.experimental import pallas as pl
from jax.experimental.pallas import tpu as pltpu
from jax.sharding import PartitionSpec as P

C = 32
GY = 32
GX = 64
ZD = 4
A_DEV = 1536
TILES = 96
TILE_A = 64
TILE_C = 512
NB = 32
NAB = 24
CELLS = GY * GX
SLABS = 16
REPS = 8
W_CHUNKS = 6
W_STEP = TILES // W_CHUNKS

UNROLL = 8
PREV_C, LAST_C, PREV_A, LAST_A, ATOM, CELL = range(6)

F32 = jnp.float32
BF16 = jnp.bfloat16
NT = (((1,), (1,)), ((), ()))
MESH = pl.DeviceIdType.MESH


def kernel(
    feats_hbm, w_hbm, atom_hbm, cell_hbm, live, mix_hbm, conv_hbm, cot_hbm,
    pot, gfe, gout,
    feats, cot, conv, mix, atom_v, cell_v, idx_v, idx,
    w, src, acc, snd_dn, snd_up, rcv_lo, rcv_hi, shifted, dside, toep1, toep2, rep1, prod, gw,
    win0, win1, cacc, gp, rs1, rs2, piece, fin,
    in_sem, w_sem, h_send, h_recv, p_send, p_recv, g_send, g_recv,
):
    slab = lax.axis_index("slab")
    rep = lax.axis_index("rep")
    up = lax.rem(slab + 1, SLABS)
    down = lax.rem(slab + SLABS - 1, SLABS)

    small = []
    pairs = ((cell_hbm, cell_v), (atom_hbm, atom_v), (feats_hbm, feats), (mix_hbm, mix),
             (conv_hbm, conv), (cot_hbm, cot))
    for k, (source, target) in enumerate(pairs):
        small.append(pltpu.make_async_copy(source, target, in_sem.at[k]))
        small[-1].start()
    loads = []
    for k in range(W_CHUNKS):
        part = pl.ds(k * W_STEP, W_STEP)
        loads.append(pltpu.make_async_copy(w_hbm.at[part], w.at[part], w_sem.at[k]))
        loads[-1].start()

    def slab_mate(k):
        return {"slab": lax.rem(slab + k, SLABS)}

    def rep_mate(k):
        return {"rep": lax.rem(rep + k, REPS)}

    mates = [slab_mate(k) for k in range(1, SLABS)] + [rep_mate(k) for k in range(1, REPS)]
    barrier = pltpu.get_barrier_semaphore()
    for mate in mates:
        pl.semaphore_signal(barrier, inc=1, device_id=mate, device_id_type=MESH)

    small[0].wait()
    small[1].wait()
    lane = lax.broadcasted_iota(jnp.int32, (TILES, TILES), 1)
    sub = lax.broadcasted_iota(jnp.int32, (TILES, TILES), 0)
    alive = sub < live[0, 0]
    number = sub + 1
    for ids, prev, last, copied, limit in (
        (cell_v, PREV_C, LAST_C, CELL, NB - 1), (atom_v, PREV_A, LAST_A, ATOM, NAB - 1)
    ):
        row = jnp.broadcast_to(ids[...], (TILES, TILES))
        column = jnp.sum(jnp.where(lane == sub, row, 0), axis=1, keepdims=True)
        before = jnp.where((column == row) & (sub < lane) & alive, number, 0)
        newest = jnp.where((column == lane) & alive, number, 0)
        idx_v[prev : prev + 1, :TILES] = jnp.clip(jnp.max(before, axis=0, keepdims=True), 0, TILES)
        idx_v[last : last + 1, :TILES] = jnp.clip(jnp.max(newest, axis=0, keepdims=True), 0, TILES)
        idx_v[copied : copied + 1, :TILES] = jnp.clip(ids[...], 0, limit)
    table = pltpu.make_async_copy(idx_v, idx, in_sem.at[6])
    table.start()

    def fill(f, values):
        for a in range(NAB):
            src[f, a] = values[:, a * TILE_A : (a + 1) * TILE_A]
        acc[f, 0] = jnp.zeros((C, TILE_C), F32)
        cacc[f, 0] = jnp.zeros((C, TILE_A), F32)

    small[2].wait()
    fill(0, feats)
    table.wait()

    def deposit(f, start, stop):
        def body(i, carry):
            first = i * UNROLL
            values = [jnp.dot(src[f, idx[ATOM, first + u]], w[first + u], preferred_element_type=F32)
                      for u in range(UNROLL)]
            for u in range(UNROLL):
                acc[f, first + u + 1] = values[u] + acc[f, idx[PREV_C, first + u]]
            return carry

        lax.fori_loop(start // UNROLL, stop // UNROLL, body, 0)

    for k in range(W_CHUNKS):
        loads[k].wait()
        deposit(0, k * W_STEP, (k + 1) * W_STEP)

    halos = []
    sides = ((snd_dn, rcv_hi, down, 0), (snd_up, rcv_lo, up, 5))

    def exchange(stage, f, wanted):
        for j in range(len(wanted[0])):
            for side, (source, target, to, base) in enumerate(sides):
                k = wanted[side][j]
                for q in range(4):
                    source[f, k, q] = acc[f, idx[LAST_C, (base + k) * 4 + q]].astype(BF16)
                copy = pltpu.make_async_remote_copy(
                    src_ref=source.at[f, k], dst_ref=target.at[f, k],
                    send_sem=h_send.at[stage, side], recv_sem=h_recv.at[stage, side],
                    device_id={"slab": to}, device_id_type=MESH)
                copy.start()
        for side, (source, target, to, base) in enumerate(sides):
            first, count = min(wanted[side]), len(wanted[side])
            halos.append(pltpu.make_async_remote_copy(
                src_ref=source.at[f, pl.ds(first, count)], dst_ref=target.at[f, pl.ds(first, count)],
                send_sem=h_send.at[stage, side], recv_sem=h_recv.at[stage, side],
                device_id={"slab": to}, device_id_type=MESH))

    pl.semaphore_wait(barrier, len(mates))
    exchange(0, 0, ((0, 1, 2), (2, 1, 0)))
    small[5].wait()
    fill(1, cot)
    deposit(1, 0, TILES)
    exchange(1, 1, ((0, 1), (2, 1)))
    exchange(2, 1, ((2,), (0,)))

    small[3].wait()
    small[4].wait()
    lane32 = lax.broadcasted_iota(jnp.int32, (C, 128), 1) // C

    def banded(toep, flip):
        for dx in range(3):
            for zo in range(4):
                for ct in range(5):
                    tile = jnp.zeros((C, 128), F32)
                    for g in range(4):
                        dy, zi = divmod(ct * 4 + g, 6)
                        if dy < 3 and 0 <= zi - zo < 3:
                            off = 9 * (zi - zo) + 3 * dy + dx
                            off = 26 - off if flip else off
                            tile = jnp.where(lane32 == g, rep1[pl.ds(off * C, C)], tile)
                    rows = slice((dx * 4 + zo) * C, (dx * 4 + zo + 1) * C)
                    width = 128 if ct < 4 else 64
                    toep[rows, ct * 128 : ct * 128 + width] = tile[:, :width].astype(BF16)

    mixing = mix[...]
    rep1[...] = jnp.dot(
        conv[...].reshape(27 * C, C), jnp.concatenate([mixing] * 4, axis=1), preferred_element_type=F32)
    banded(toep1, False)
    mix_t = mixing.astype(F32).T.astype(BF16)

    for off in range(27):
        wide = jnp.concatenate([conv[off]] * 4, axis=0)
        rep1[off * C : (off + 1) * C] = lax.dot_general(mix_t, wide, NT, preferred_element_type=F32)
    banded(toep2, True)

    spot = lax.broadcasted_iota(jnp.int32, (128, 128), 1)
    first_x = lax.rem(spot, GX) == 0
    last_x = lax.rem(spot, GX) == GX - 1

    low_half = spot[:C] < GX

    def next_x(v):
        return jnp.where(last_x, pltpu.roll(v, GX - 1, 1), pltpu.roll(v, 127, 1))

    def prev_x(v):
        return jnp.where(first_x, pltpu.roll(v, 128 - GX + 1, 1), pltpu.roll(v, 1, 1))

    def stack(f, p):
        got = rcv_lo.at[f, p] if p < 3 else rcv_hi.at[f, p - 3]
        plane = jnp.concatenate(
            [acc[f, idx[LAST_C, (p + 1) * 4 + q]] + got[q].astype(F32) for q in range(4)], axis=1)
        own = slice(p * C, (p + 1) * C)
        shifted[f, 1, own] = plane.astype(BF16)
        turned = [pltpu.roll(plane[:, k * 128 : (k + 1) * 128], GX, 1) for k in range(16)]
        for k in range(16):
            cols = slice(k * 128, (k + 1) * 128)
            shifted[f, 0, own, cols] = jnp.where(low_half, turned[k - 1], turned[k]).astype(BF16)
            shifted[f, 2, own, cols] = jnp.where(low_half, turned[k], turned[(k + 1) % 16]).astype(BF16)

    phis = []
    win = (win0, win1)

    def convolve(f):
        toep = toep2 if f else toep1
        for q in range(4):
            cols = slice(q * TILE_C, (q + 1) * TILE_C)
            stacked = shifted[f, :, :, cols].reshape(18 * C, TILE_C)
            prod[...] = jnp.dot(toep[...], stacked, preferred_element_type=F32)
            for h in range(4):
                part = slice(h * 128, (h + 1) * 128)
                low, mid, high = (prod[d * 128 : (d + 1) * 128, part] for d in range(3))
                phi = (mid + prev_x(low) + next_x(high)).astype(BF16)
                for z in range(ZD):
                    win[f][(z + 2) * 4 + q, :, part] = phi[z * C : (z + 1) * C]
        for side, (start, land, to) in enumerate(((8, 24, down), (16, 0, up))):
            phis.append(pltpu.make_async_remote_copy(
                src_ref=win[f].at[pl.ds(start, 8)], dst_ref=win[f].at[pl.ds(land, 8)],
                send_sem=p_send.at[f, side], recv_sem=p_recv.at[f, side],
                device_id={"slab": to}, device_id_type=MESH))
            phis[-1].start()

    halos[0].wait_recv()
    halos[1].wait_recv()
    for p in range(6):
        stack(0, p)
    convolve(0)

    halos[2].wait_recv()
    halos[3].wait_recv()
    for p in range(1, 5):
        stack(1, p)
    for k in range(16):
        cols = slice(k * 128, (k + 1) * 128)
        v = shifted[1, 1, C : 5 * C, cols].astype(F32)
        for dx, moved in enumerate((next_x(v), v, prev_x(v))):
            for z in range(ZD):
                dside[z, dx * C : (dx + 1) * C, cols] = moved[z * C : (z + 1) * C].astype(BF16)
    for dy in range(3):
        total = None
        for z in range(ZD):
            part = lax.dot_general(dside[z], shifted[0, dy, z * C : (z + 3) * C], NT, preferred_element_type=F32)
            total = part if total is None else total + part
        gw[:, dy * 3 * C : (dy + 1) * 3 * C] = total
    for half in range(2):
        gp[half * 6 : (half + 1) * 6] = gw[:, half * 128 : (half + 1) * 128].reshape(6, C // 2, 128)
    gp[12:] = jnp.zeros((4, C // 2, 128), F32)
    for dx in range(3):
        gp[12:14, :, dx * C : (dx + 1) * C] = gw[dx * C : (dx + 1) * C, 256:].reshape(2, C // 2, C)

    def give(source, target, phase, mate):
        pltpu.make_async_remote_copy(
            src_ref=source, dst_ref=target, send_sem=g_send.at[phase], recv_sem=g_recv.at[phase],
            device_id=mate, device_id_type=MESH).start()

    def all_of(buffer, count, phase):
        part = buffer.at[pl.ds(0, count)]
        return pltpu.make_async_remote_copy(
            src_ref=part, dst_ref=part, send_sem=g_send.at[phase], recv_sem=g_recv.at[phase],
            device_id=slab_mate(1), device_id_type=MESH)

    for k in range(1, SLABS):
        give(gp.at[lax.rem(slab + k, SLABS)], rs1.at[k], 0, slab_mate(k))
    rs1[0] = gp[slab]

    halos[4].wait_recv()
    halos[5].wait_recv()
    stack(1, 0)
    stack(1, 5)
    convolve(1)

    all_of(rs1, SLABS - 1, 0).wait_recv()
    piece[...] = jnp.sum(rs1[...], axis=0)
    for k in range(1, REPS):
        give(piece, rs2.at[rep], 1, rep_mate(k))
    rs2[rep] = piece[...]

    def collect(f):
        def body(i, carry):
            first = i * UNROLL
            values = [lax.dot_general(win[f][idx[CELL, first + u]], w[first + u], NT, preferred_element_type=F32)
                      for u in range(UNROLL)]
            for u in range(UNROLL):
                cacc[f, first + u + 1] = values[u] + cacc[f, idx[PREV_A, first + u]]
            return carry

        lax.fori_loop(0, TILES // UNROLL, body, 0)
        out = gfe if f else pot
        for a in range(0, NAB, 2):
            pair = jnp.concatenate([cacc[f, idx[LAST_A, a]], cacc[f, idx[LAST_A, a + 1]]], axis=1)
            out[:, a * TILE_A : (a + 2) * TILE_A] = pair.astype(BF16)

    phis[0].wait_recv()
    phis[1].wait_recv()
    collect(0)

    all_of(rs2, REPS - 1, 1).wait_recv()
    fin[...] = jnp.sum(rs2[...], axis=0)
    for k in range(1, SLABS):
        give(fin, gout.at[slab], 2, slab_mate(k))
    gout[slab] = fin[...]

    phis[2].wait_recv()
    phis[3].wait_recv()
    collect(1)

    all_of(rs1, SLABS - 1, 0).wait_send()
    all_of(rs2, REPS - 1, 1).wait_send()
    for copy in halos + phis:
        copy.wait_send()
    all_of(rs1, SLABS - 1, 2).wait_send()
    all_of(rs1, SLABS - 1, 2).wait_recv()


def finish(pot_in, gfe_in, moments, mix_hbm, conv_hbm, pot, gfe, gconv, gmix, mix, conv, flat, sem):
    copies = [pltpu.make_async_copy(mix_hbm, mix, sem.at[0]), pltpu.make_async_copy(conv_hbm, conv, sem.at[1]),
              pltpu.make_async_copy(pot_in, pot, sem.at[2]), pltpu.make_async_copy(gfe_in, gfe, sem.at[3])]
    for copy in copies:
        copy.start()
    for off in range(27):
        dz, dy, dx = off // 9, off // 3 % 3, off % 3
        group = dy * 3 + dz
        first, place = (group // 4 * 6 + dx * 2, group % 4) if group < 8 else (12, dx)
        part = moments[first : first + 2, :, place * C : (place + 1) * C]
        flat[off * C : (off + 1) * C] = part.reshape(C, C)
    copies[0].wait()
    copies[1].wait()
    value = flat[...]
    high = value.astype(BF16)
    low = (value - high.astype(F32)).astype(BF16)
    mixing = mix[...]
    turned = conv[...].reshape(27 * C, C).astype(F32).T.astype(BF16)
    devices = REPS * SLABS
    conv_scale = 1.0 / math.sqrt(devices * ZD * GY * GX)
    mix_scale = 1.0 / math.sqrt(devices * A_DEV)
    product = (lax.dot_general(high, mixing, NT, preferred_element_type=F32)
               + lax.dot_general(low, mixing, NT, preferred_element_type=F32))
    gconv[...] = (product * conv_scale).reshape(27, C, C)
    gmix[...] = (jnp.dot(turned, high, preferred_element_type=F32)
                 + jnp.dot(turned, low, preferred_element_type=F32)) * mix_scale
    copies[2].wait()
    copies[3].wait()


def local(feats, tile_weight, tile_atom, tile_cell, tile_live, w_mix, conv_w, cotangent):
    vmem = pl.BlockSpec(memory_space=pltpu.VMEM)
    hbm = pl.BlockSpec(memory_space=pltpu.HBM)
    dma = pltpu.SemaphoreType.DMA
    field = jax.ShapeDtypeStruct((C, A_DEV), BF16)
    pot, gfe, total = pl.pallas_call(
        kernel,
        out_shape=(pltpu.VMEM((C, A_DEV), BF16), pltpu.VMEM((C, A_DEV), BF16), pltpu.VMEM((SLABS, C // 2, 128), F32)),
        in_specs=[hbm] * 4 + [pl.BlockSpec(memory_space=pltpu.SMEM)] + [hbm] * 3,
        out_specs=(vmem, vmem, vmem),
        scratch_shapes=[
            pltpu.VMEM((C, A_DEV), BF16),
            pltpu.VMEM((C, A_DEV), BF16),
            pltpu.VMEM((27, C, C), BF16),
            pltpu.VMEM((C, C), BF16),
            pltpu.VMEM((1, TILES), jnp.int32),
            pltpu.VMEM((1, TILES), jnp.int32),
            pltpu.VMEM((8, 128), jnp.int32),
            pltpu.SMEM((8, 128), jnp.int32),
            pltpu.VMEM((TILES, TILE_A, TILE_C), BF16),
            pltpu.VMEM((2, NAB, C, TILE_A), BF16),
            pltpu.VMEM((2, TILES + 1, C, TILE_C), F32),
            pltpu.VMEM((2, 3, 4, C, TILE_C), BF16),
            pltpu.VMEM((2, 3, 4, C, TILE_C), BF16),
            pltpu.VMEM((2, 3, 4, C, TILE_C), BF16),
            pltpu.VMEM((2, 3, 4, C, TILE_C), BF16),
            pltpu.VMEM((2, 3, 6 * C, CELLS), BF16),
            pltpu.VMEM((ZD, 3 * C, CELLS), BF16),
            pltpu.VMEM((12 * C, 18 * C), BF16),
            pltpu.VMEM((12 * C, 18 * C), BF16),
            pltpu.VMEM((27 * C, 128), F32),
            pltpu.VMEM((12 * C, TILE_C), F32),
            pltpu.VMEM((3 * C, 9 * C), F32),
            pltpu.VMEM((NB, C, TILE_C), BF16),
            pltpu.VMEM((NB, C, TILE_C), BF16),
            pltpu.VMEM((2, TILES + 1, C, TILE_A), F32),
            pltpu.VMEM((SLABS, C // 2, 128), F32),
            pltpu.VMEM((SLABS, C // 2, 128), F32),
            pltpu.VMEM((REPS, C // 2, 128), F32),
            pltpu.VMEM((C // 2, 128), F32),
            pltpu.VMEM((C // 2, 128), F32),
            dma((7,)), dma((W_CHUNKS,)), dma((3, 2)), dma((3, 2)), dma((2, 2)), dma((2, 2)), dma((3,)), dma((3,)),
        ],
        compiler_params=pltpu.CompilerParams(
            collective_id=0, has_side_effects=True, vmem_limit_bytes=56 * 2**20,
        ),
    )(feats[0], tile_weight[0], tile_atom, tile_cell, tile_live, w_mix, conv_w, cotangent[0])
    pot, gfe, gconv, gmix = pl.pallas_call(
        finish,
        out_shape=(field, field, jax.ShapeDtypeStruct((27, C, C), F32), jax.ShapeDtypeStruct((C, C), F32)),
        in_specs=[vmem, vmem, vmem, hbm, hbm],
        out_specs=(hbm, hbm, vmem, vmem),
        scratch_shapes=[
            pltpu.VMEM((C, C), BF16),
            pltpu.VMEM((27, C, C), BF16),
            pltpu.VMEM((27 * C, C), F32),
            dma((4,)),
        ],
    )(pot, gfe, total, w_mix, conv_w)
    return pot[None], gfe[None], gconv, gmix


def solution(mesh):
    return jax.shard_map(
        local,
        mesh=mesh,
        in_specs=(
            P("rep", None, "slab"),
            P("rep", "slab", None, None),
            P("rep", "slab"),
            P("rep", "slab"),
            P("rep", "slab"),
            P(),
            P(),
            P("rep", None, "slab"),
        ),
        out_specs=(P("rep", None, "slab"), P("rep", None, "slab"), P(), P()),
        check_vma=False,
    )
```

```python
import math

import jax
import jax.numpy as jnp
from jax import lax
from jax.experimental import pallas as pl
from jax.experimental.pallas import tpu as pltpu
from jax.sharding import PartitionSpec as P

C = 32
GY = 32
GX = 64
ZD = 4
A_DEV = 1536
TILES = 96
TILE_A = 64
TILE_C = 512
NB = 32
NAB = 24
CELLS = GY * GX
SLABS = 16
REPS = 8
W_CHUNKS = 6
W_STEP = TILES // W_CHUNKS

UNROLL = 8
GROUP = 16
ROW = 8
PREV_C, LAST_C, PREV_A, LAST_A, ATOM, CELL = range(6)

F32 = jnp.float32
BF16 = jnp.bfloat16
NT = (((1,), (1,)), ((), ()))
MESH = pl.DeviceIdType.MESH


def kernel(
    feats_hbm, w_hbm, atom_hbm, cell_hbm, live, mix_hbm, conv_hbm, cot_hbm,
    pot, gfe, gout,
    pot_v, gfe_v, feats, cot, conv, mix, atom_v, cell_v, idx_v, idx,
    w, src, acc, snd_dn, snd_up, rcv_lo, rcv_hi, shifted, dside, toep1, toep2, rep1, prod, gw,
    win0, win1, cacc, gp, rs1, rs2, piece, fin,
    in_sem, out_sem, w_sem, h_send, h_recv, p_send, p_recv, g_send, g_recv,
):
    slab = lax.axis_index("slab")
    rep = lax.axis_index("rep")
    chip, core = slab // 2, lax.rem(slab, 2)
    member = rep * 2 + core
    up = lax.rem(slab + 1, SLABS)
    down = lax.rem(slab + SLABS - 1, SLABS)

    small = []
    pairs = ((cell_hbm, cell_v), (atom_hbm, atom_v), (feats_hbm, feats), (mix_hbm, mix),
             (conv_hbm, conv), (cot_hbm, cot))
    for k, (source, target) in enumerate(pairs):
        small.append(pltpu.make_async_copy(source, target, in_sem.at[k]))
        small[-1].start()
    loads = []
    for k in range(W_CHUNKS):
        part = pl.ds(k * W_STEP, W_STEP)
        loads.append(pltpu.make_async_copy(w_hbm.at[part], w.at[part], w_sem.at[k]))
        loads[-1].start()

    def plane_mate(k):
        other = lax.rem(member + k, GROUP)
        return {"rep": other // 2, "slab": chip * 2 + lax.rem(other, 2)}

    def row_mate(k):
        return {"slab": lax.rem(chip + k, ROW) * 2 + core}

    mates = [plane_mate(k) for k in range(1, GROUP)] + [row_mate(k) for k in range(1, ROW)]
    mates += [{"slab": up}, {"slab": down}]
    barrier = pltpu.get_barrier_semaphore()
    for mate in mates:
        pl.semaphore_signal(barrier, inc=1, device_id=mate, device_id_type=MESH)

    small[0].wait()
    small[1].wait()
    lane = lax.broadcasted_iota(jnp.int32, (TILES, TILES), 1)
    sub = lax.broadcasted_iota(jnp.int32, (TILES, TILES), 0)
    alive = sub < live[0, 0]
    number = sub + 1
    for ids, prev, last, copied, limit in (
        (cell_v, PREV_C, LAST_C, CELL, NB - 1), (atom_v, PREV_A, LAST_A, ATOM, NAB - 1)
    ):
        row = jnp.broadcast_to(ids[...], (TILES, TILES))
        column = jnp.sum(jnp.where(lane == sub, row, 0), axis=1, keepdims=True)
        before = jnp.where((column == row) & (sub < lane) & alive, number, 0)
        newest = jnp.where((column == lane) & alive, number, 0)
        idx_v[prev : prev + 1, :TILES] = jnp.clip(jnp.max(before, axis=0, keepdims=True), 0, TILES)
        idx_v[last : last + 1, :TILES] = jnp.clip(jnp.max(newest, axis=0, keepdims=True), 0, TILES)
        idx_v[copied : copied + 1, :TILES] = jnp.clip(ids[...], 0, limit)
    table = pltpu.make_async_copy(idx_v, idx, in_sem.at[6])
    table.start()

    def fill(f, values):
        for a in range(NAB):
            src[f, a] = values[:, a * TILE_A : (a + 1) * TILE_A]
        acc[f, 0] = jnp.zeros((C, TILE_C), F32)
        cacc[f, 0] = jnp.zeros((C, TILE_A), F32)

    small[2].wait()
    fill(0, feats)
    table.wait()

    def deposit(f, start, stop):
        def body(i, carry):
            first = i * UNROLL
            values = [jnp.dot(src[f, idx[ATOM, first + u]], w[first + u], preferred_element_type=F32)
                      for u in range(UNROLL)]
            for u in range(UNROLL):
                acc[f, first + u + 1] = values[u] + acc[f, idx[PREV_C, first + u]]
            return carry

        lax.fori_loop(start // UNROLL, stop // UNROLL, body, 0)

    for k in range(W_CHUNKS):
        loads[k].wait()
        deposit(0, k * W_STEP, (k + 1) * W_STEP)

    halos = []
    sides = ((snd_dn, rcv_hi, down, 0), (snd_up, rcv_lo, up, 5))

    def exchange(stage, f, wanted):
        for j in range(len(wanted[0])):
            for side, (source, target, to, base) in enumerate(sides):
                k = wanted[side][j]
                for q in range(4):
                    source[f, k, q] = acc[f, idx[LAST_C, (base + k) * 4 + q]].astype(BF16)
                copy = pltpu.make_async_remote_copy(
                    src_ref=source.at[f, k], dst_ref=target.at[f, k],
                    send_sem=h_send.at[stage, side], recv_sem=h_recv.at[stage, side],
                    device_id={"slab": to}, device_id_type=MESH)
                copy.start()
        for side, (source, target, to, base) in enumerate(sides):
            first, count = min(wanted[side]), len(wanted[side])
            halos.append(pltpu.make_async_remote_copy(
                src_ref=source.at[f, pl.ds(first, count)], dst_ref=target.at[f, pl.ds(first, count)],
                send_sem=h_send.at[stage, side], recv_sem=h_recv.at[stage, side],
                device_id={"slab": to}, device_id_type=MESH))

    pl.semaphore_wait(barrier, len(mates))
    exchange(0, 0, ((0, 1, 2), (2, 1, 0)))
    small[5].wait()
    fill(1, cot)
    deposit(1, 0, TILES)
    exchange(1, 1, ((0, 1), (2, 1)))
    exchange(2, 1, ((2,), (0,)))

    small[3].wait()
    small[4].wait()
    lane32 = lax.broadcasted_iota(jnp.int32, (C, 128), 1) // C

    def banded(toep, flip):
        for dx in range(3):
            for zo in range(4):
                for ct in range(5):
                    tile = jnp.zeros((C, 128), F32)
                    for g in range(4):
                        dy, zi = divmod(ct * 4 + g, 6)
                        if dy < 3 and 0 <= zi - zo < 3:
                            off = 9 * (zi - zo) + 3 * dy + dx
                            off = 26 - off if flip else off
                            tile = jnp.where(lane32 == g, rep1[pl.ds(off * C, C)], tile)
                    rows = slice((dx * 4 + zo) * C, (dx * 4 + zo + 1) * C)
                    width = 128 if ct < 4 else 64
                    toep[rows, ct * 128 : ct * 128 + width] = tile[:, :width].astype(BF16)

    mixing = mix[...]
    rep1[...] = jnp.dot(
        conv[...].reshape(27 * C, C), jnp.concatenate([mixing] * 4, axis=1), preferred_element_type=F32)
    banded(toep1, False)
    mix_t = mixing.astype(F32).T.astype(BF16)

    for off in range(27):
        wide = jnp.concatenate([conv[off]] * 4, axis=0)
        rep1[off * C : (off + 1) * C] = lax.dot_general(mix_t, wide, NT, preferred_element_type=F32)
    banded(toep2, True)

    spot = lax.broadcasted_iota(jnp.int32, (128, 128), 1)
    first_x = lax.rem(spot, GX) == 0
    last_x = lax.rem(spot, GX) == GX - 1

    low_half = spot[:C] < GX

    def next_x(v):
        return jnp.where(last_x, pltpu.roll(v, GX - 1, 1), pltpu.roll(v, 127, 1))

    def prev_x(v):
        return jnp.where(first_x, pltpu.roll(v, 128 - GX + 1, 1), pltpu.roll(v, 1, 1))

    def stack(f, p):
        got = rcv_lo.at[f, p] if p < 3 else rcv_hi.at[f, p - 3]
        plane = jnp.concatenate(
            [acc[f, idx[LAST_C, (p + 1) * 4 + q]] + got[q].astype(F32) for q in range(4)], axis=1)
        own = slice(p * C, (p + 1) * C)
        shifted[f, 1, own] = plane.astype(BF16)
        turned = [pltpu.roll(plane[:, k * 128 : (k + 1) * 128], GX, 1) for k in range(16)]
        for k in range(16):
            cols = slice(k * 128, (k + 1) * 128)
            shifted[f, 0, own, cols] = jnp.where(low_half, turned[k - 1], turned[k]).astype(BF16)
            shifted[f, 2, own, cols] = jnp.where(low_half, turned[k], turned[(k + 1) % 16]).astype(BF16)

    phis = []
    win = (win0, win1)

    def convolve(f, before_send):
        toep = toep2 if f else toep1
        for q in range(4):
            cols = slice(q * TILE_C, (q + 1) * TILE_C)
            stacked = shifted[f, :, :, cols].reshape(18 * C, TILE_C)
            prod[...] = jnp.dot(toep[...], stacked, preferred_element_type=F32)
            for h in range(4):
                part = slice(h * 128, (h + 1) * 128)
                low, mid, high = (prod[d * 128 : (d + 1) * 128, part] for d in range(3))
                phi = (mid + prev_x(low) + next_x(high)).astype(BF16)
                for z in range(ZD):
                    win[f][(z + 2) * 4 + q, :, part] = phi[z * C : (z + 1) * C]
        before_send()
        for side, (start, land, to) in enumerate(((8, 24, down), (16, 0, up))):
            phis.append(pltpu.make_async_remote_copy(
                src_ref=win[f].at[pl.ds(start, 8)], dst_ref=win[f].at[pl.ds(land, 8)],
                send_sem=p_send.at[f, side], recv_sem=p_recv.at[f, side],
                device_id={"slab": to}, device_id_type=MESH))
            phis[-1].start()

    halos[0].wait_recv()
    halos[1].wait_recv()
    for p in range(6):
        stack(0, p)
    convolve(0, lambda: None)

    halos[2].wait_recv()
    halos[3].wait_recv()
    for p in range(1, 5):
        stack(1, p)
    for k in range(16):
        cols = slice(k * 128, (k + 1) * 128)
        v = shifted[1, 1, C : 5 * C, cols].astype(F32)
        for dx, moved in enumerate((next_x(v), v, prev_x(v))):
            for z in range(ZD):
                dside[z, dx * C : (dx + 1) * C, cols] = moved[z * C : (z + 1) * C].astype(BF16)
    for dy in range(3):
        total = None
        for z in range(ZD):
            part = lax.dot_general(dside[z], shifted[0, dy, z * C : (z + 3) * C], NT, preferred_element_type=F32)
            total = part if total is None else total + part
        gw[:, dy * 3 * C : (dy + 1) * 3 * C] = total
    for half in range(2):
        gp[half * 6 : (half + 1) * 6] = gw[:, half * 128 : (half + 1) * 128].reshape(6, C // 2, 128)
    gp[12:] = jnp.zeros((4, C // 2, 128), F32)
    for dx in range(3):
        gp[12:14, :, dx * C : (dx + 1) * C] = gw[dx * C : (dx + 1) * C, 256:].reshape(2, C // 2, C)

    def give(source, target, phase, mate):
        pltpu.make_async_remote_copy(
            src_ref=source, dst_ref=target, send_sem=g_send.at[phase], recv_sem=g_recv.at[phase],
            device_id=mate, device_id_type=MESH).start()

    def all_of(buffer, count, phase):
        part = buffer.at[pl.ds(0, count)]
        return pltpu.make_async_remote_copy(
            src_ref=part, dst_ref=part, send_sem=g_send.at[phase], recv_sem=g_recv.at[phase],
            device_id=plane_mate(1), device_id_type=MESH)

    for k in range(1, GROUP):
        give(gp.at[lax.rem(member + k, GROUP)], rs1.at[k], 0, plane_mate(k))
    rs1[0] = gp[member]

    def middle():
        all_of(rs1, GROUP - 1, 0).wait_recv()
        piece[...] = jnp.sum(rs1[...], axis=0)
        for k in range(1, ROW):
            give(piece, rs2.at[chip], 1, row_mate(k))
        rs2[chip] = piece[...]

    halos[4].wait_recv()
    halos[5].wait_recv()
    stack(1, 0)
    stack(1, 5)
    convolve(1, middle)

    def collect(f):
        def body(i, carry):
            first = i * UNROLL
            values = [lax.dot_general(win[f][idx[CELL, first + u]], w[first + u], NT, preferred_element_type=F32)
                      for u in range(UNROLL)]
            for u in range(UNROLL):
                cacc[f, first + u + 1] = values[u] + cacc[f, idx[PREV_A, first + u]]
            return carry

        lax.fori_loop(0, TILES // UNROLL, body, 0)
        out_v, out = (gfe_v, gfe) if f else (pot_v, pot)
        for a in range(0, NAB, 2):
            pair = jnp.concatenate([cacc[f, idx[LAST_A, a]], cacc[f, idx[LAST_A, a + 1]]], axis=1)
            out_v[:, a * TILE_A : (a + 2) * TILE_A] = pair.astype(BF16)
        copy = pltpu.make_async_copy(out_v, out, out_sem.at[f])
        copy.start()
        return copy

    phis[0].wait_recv()
    phis[1].wait_recv()
    outs = [collect(0)]

    all_of(rs2, ROW - 1, 1).wait_recv()
    fin[...] = jnp.sum(rs2[...], axis=0)
    for k in range(1, GROUP):
        give(fin, gout.at[member], 2, plane_mate(k))
    outs.append(pltpu.make_async_copy(fin, gout.at[member], out_sem.at[2]))
    outs[-1].start()

    phis[2].wait_recv()
    phis[3].wait_recv()
    outs.append(collect(1))

    all_of(rs1, GROUP - 1, 0).wait_send()
    all_of(rs2, ROW - 1, 1).wait_send()
    for copy in halos + phis:
        copy.wait_send()
    all_of(rs1, GROUP - 1, 2).wait_send()
    all_of(rs1, GROUP - 1, 2).wait_recv()
    for copy in outs:
        copy.wait()


def finish(pot_in, gfe_in, moments_hbm, mix_hbm, conv_hbm, pot, gfe, gconv, gmix, moments, mix, conv, flat, sem):
    pairs = ((moments_hbm, moments), (mix_hbm, mix), (conv_hbm, conv), (pot_in, pot), (gfe_in, gfe))
    copies = [pltpu.make_async_copy(source, target, sem.at[k]) for k, (source, target) in enumerate(pairs)]
    for copy in copies:
        copy.start()
    for copy in copies[:3]:
        copy.wait()
    for off in range(27):
        dz, dy, dx = off // 9, off // 3 % 3, off % 3
        group = dy * 3 + dz
        first, place = (group // 4 * 6 + dx * 2, group % 4) if group < 8 else (12, dx)
        part = moments[first : first + 2, :, place * C : (place + 1) * C]
        flat[off * C : (off + 1) * C] = part.reshape(C, C)
    value = flat[...]
    high = value.astype(BF16)
    low = (value - high.astype(F32)).astype(BF16)
    mixing = mix[...]
    turned = conv[...].reshape(27 * C, C).astype(F32).T.astype(BF16)
    devices = REPS * SLABS
    conv_scale = 1.0 / math.sqrt(devices * ZD * GY * GX)
    mix_scale = 1.0 / math.sqrt(devices * A_DEV)
    product = (lax.dot_general(high, mixing, NT, preferred_element_type=F32)
               + lax.dot_general(low, mixing, NT, preferred_element_type=F32))
    gconv[...] = (product * conv_scale).reshape(27, C, C)
    gmix[...] = (jnp.dot(turned, high, preferred_element_type=F32)
                 + jnp.dot(turned, low, preferred_element_type=F32)) * mix_scale
    for copy in copies[3:]:
        copy.wait()


def local(feats, tile_weight, tile_atom, tile_cell, tile_live, w_mix, conv_w, cotangent):
    vmem = pl.BlockSpec(memory_space=pltpu.VMEM)
    hbm = pl.BlockSpec(memory_space=pltpu.HBM)
    dma = pltpu.SemaphoreType.DMA
    field = jax.ShapeDtypeStruct((C, A_DEV), BF16)
    pot, gfe, total = pl.pallas_call(
        kernel,
        out_shape=(field, field, jax.ShapeDtypeStruct((GROUP, C // 2, 128), F32)),
        in_specs=[hbm] * 4 + [pl.BlockSpec(memory_space=pltpu.SMEM)] + [hbm] * 3,
        out_specs=(hbm, hbm, hbm),
        scratch_shapes=[
            pltpu.VMEM((C, A_DEV), BF16),
            pltpu.VMEM((C, A_DEV), BF16),
            pltpu.VMEM((C, A_DEV), BF16),
            pltpu.VMEM((C, A_DEV), BF16),
            pltpu.VMEM((27, C, C), BF16),
            pltpu.VMEM((C, C), BF16),
            pltpu.VMEM((1, TILES), jnp.int32),
            pltpu.VMEM((1, TILES), jnp.int32),
            pltpu.VMEM((8, 128), jnp.int32),
            pltpu.SMEM((8, 128), jnp.int32),
            pltpu.VMEM((TILES, TILE_A, TILE_C), BF16),
            pltpu.VMEM((2, NAB, C, TILE_A), BF16),
            pltpu.VMEM((2, TILES + 1, C, TILE_C), F32),
            pltpu.VMEM((2, 3, 4, C, TILE_C), BF16),
            pltpu.VMEM((2, 3, 4, C, TILE_C), BF16),
            pltpu.VMEM((2, 3, 4, C, TILE_C), BF16),
            pltpu.VMEM((2, 3, 4, C, TILE_C), BF16),
            pltpu.VMEM((2, 3, 6 * C, CELLS), BF16),
            pltpu.VMEM((ZD, 3 * C, CELLS), BF16),
            pltpu.VMEM((12 * C, 18 * C), BF16),
            pltpu.VMEM((12 * C, 18 * C), BF16),
            pltpu.VMEM((27 * C, 128), F32),
            pltpu.VMEM((12 * C, TILE_C), F32),
            pltpu.VMEM((3 * C, 9 * C), F32),
            pltpu.VMEM((NB, C, TILE_C), BF16),
            pltpu.VMEM((NB, C, TILE_C), BF16),
            pltpu.VMEM((2, TILES + 1, C, TILE_A), F32),
            pltpu.VMEM((GROUP, C // 2, 128), F32),
            pltpu.VMEM((GROUP, C // 2, 128), F32),
            pltpu.VMEM((ROW, C // 2, 128), F32),
            pltpu.VMEM((C // 2, 128), F32),
            pltpu.VMEM((C // 2, 128), F32),
            dma((7,)), dma((3,)), dma((W_CHUNKS,)), dma((3, 2)), dma((3, 2)), dma((2, 2)), dma((2, 2)), dma((3,)), dma((3,)),
        ],
        compiler_params=pltpu.CompilerParams(
            collective_id=0, has_side_effects=True, vmem_limit_bytes=56 * 2**20,
        ),
    )(feats[0], tile_weight[0], tile_atom, tile_cell, tile_live, w_mix, conv_w, cotangent[0])
    pot, gfe, gconv, gmix = pl.pallas_call(
        finish,
        out_shape=(field, field, jax.ShapeDtypeStruct((27, C, C), F32), jax.ShapeDtypeStruct((C, C), F32)),
        in_specs=[hbm] * 5,
        out_specs=(vmem,) * 4,
        scratch_shapes=[
            pltpu.VMEM((GROUP, C // 2, 128), F32),
            pltpu.VMEM((C, C), BF16),
            pltpu.VMEM((27, C, C), BF16),
            pltpu.VMEM((27 * C, C), F32),
            dma((5,)),
        ],
    )(pot, gfe, total, w_mix, conv_w)
    return pot[None], gfe[None], gconv, gmix


def solution(mesh):
    return jax.shard_map(
        local,
        mesh=mesh,
        in_specs=(
            P("rep", None, "slab"),
            P("rep", "slab", None, None),
            P("rep", "slab"),
            P("rep", "slab"),
            P("rep", "slab"),
            P(),
            P(),
            P("rep", None, "slab"),
        ),
        out_specs=(P("rep", None, "slab"), P("rep", None, "slab"), P(), P()),
        check_vma=False,
    )
```

```python
import math

import jax
import jax.numpy as jnp
from jax import lax
from jax.experimental import pallas as pl
from jax.experimental.pallas import tpu as pltpu
from jax.sharding import PartitionSpec as P

C = 32
GY = 32
GX = 64
ZD = 4
A_DEV = 1536
TILES = 96
TILE_A = 64
TILE_C = 512
NB = 32
NAB = 24
CELLS = GY * GX
SLABS = 16
REPS = 8
W_CHUNKS = 4
W_STEP = TILES // W_CHUNKS

UNROLL = 24
GROUP = 16
ROW = 8
PREV_C, LAST_C, PREV_A, LAST_A, ATOM, CELL = range(6)

F32 = jnp.float32
BF16 = jnp.bfloat16
NT = (((1,), (1,)), ((), ()))
MESH = pl.DeviceIdType.MESH


def kernel(
    feats_hbm, w_hbm, atom_hbm, cell_hbm, live, mix_hbm, conv_hbm, cot_hbm,
    pot, gfe, gout,
    pot_v, gfe_v, feats, cot, conv, mix, atom_v, cell_v, idx_v, idx,
    w, src, acc, snd_dn, snd_up, rcv_lo, rcv_hi, shifted, dside, toep1, toep2, rep1, prod, gw,
    win0, win1, cacc, gp, rs1, rs2, piece, fin,
    in_sem, out_sem, w_sem, h_send, h_recv, p_send, p_recv, g_send, g_recv,
):
    slab = lax.axis_index("slab")
    rep = lax.axis_index("rep")
    chip, core = slab // 2, lax.rem(slab, 2)
    member = rep * 2 + core
    up = lax.rem(slab + 1, SLABS)
    down = lax.rem(slab + SLABS - 1, SLABS)

    small = []
    pairs = ((cell_hbm, cell_v), (atom_hbm, atom_v), (feats_hbm, feats), (mix_hbm, mix),
             (conv_hbm, conv), (cot_hbm, cot))
    for k, (source, target) in enumerate(pairs):
        small.append(pltpu.make_async_copy(source, target, in_sem.at[k]))
        small[-1].start()
    loads = []
    for k in range(W_CHUNKS):
        part = pl.ds(k * W_STEP, W_STEP)
        loads.append(pltpu.make_async_copy(w_hbm.at[part], w.at[part], w_sem.at[k]))
        loads[-1].start()

    def plane_mate(k):
        other = lax.rem(member + k, GROUP)
        return {"rep": other // 2, "slab": chip * 2 + lax.rem(other, 2)}

    def row_mate(k):
        return {"slab": lax.rem(chip + k, ROW) * 2 + core}

    plane_mates = [plane_mate(k) for k in range(1, GROUP)]
    row_mates = [row_mate(k) for k in range(1, ROW)]
    mates = plane_mates + row_mates + [{"slab": up}, {"slab": down}]
    barrier = pltpu.get_barrier_semaphore()
    for mate in mates:
        pl.semaphore_signal(barrier, inc=1, device_id=mate, device_id_type=MESH)

    small[0].wait()
    small[1].wait()
    lane = lax.broadcasted_iota(jnp.int32, (TILES, TILES), 1)
    sub = lax.broadcasted_iota(jnp.int32, (TILES, TILES), 0)
    alive = sub < live[0, 0]
    number = sub + 1
    for ids, prev, last, copied, limit in (
        (cell_v, PREV_C, LAST_C, CELL, NB - 1), (atom_v, PREV_A, LAST_A, ATOM, NAB - 1)
    ):
        row = jnp.broadcast_to(ids[...], (TILES, TILES))
        column = jnp.sum(jnp.where(lane == sub, row, 0), axis=1, keepdims=True)
        before = jnp.where((column == row) & (sub < lane) & alive, number, 0)
        newest = jnp.where((column == lane) & alive, number, 0)
        idx_v[prev : prev + 1, :TILES] = jnp.clip(jnp.max(before, axis=0, keepdims=True), 0, TILES)
        idx_v[last : last + 1, :TILES] = jnp.clip(jnp.max(newest, axis=0, keepdims=True), 0, TILES)
        idx_v[copied : copied + 1, :TILES] = jnp.clip(ids[...], 0, limit)
    table = pltpu.make_async_copy(idx_v, idx, in_sem.at[6])
    table.start()

    def fill(f, values):
        for a in range(NAB):
            src[f, a] = values[:, a * TILE_A : (a + 1) * TILE_A]
        acc[f, 0] = jnp.zeros((C, TILE_C), F32)
        cacc[f, 0] = jnp.zeros((C, TILE_A), F32)

    small[2].wait()
    fill(0, feats)
    table.wait()

    def deposit(f, start, stop):
        def body(i, carry):
            first = i * UNROLL
            values = [jnp.dot(src[f, idx[ATOM, first + u]], w[first + u], preferred_element_type=F32)
                      for u in range(UNROLL)]
            for u in range(UNROLL):
                acc[f, first + u + 1] = values[u] + acc[f, idx[PREV_C, first + u]]
            return carry

        lax.fori_loop(start // UNROLL, stop // UNROLL, body, 0)

    for k in range(W_CHUNKS):
        loads[k].wait()
        deposit(0, k * W_STEP, (k + 1) * W_STEP)

    halos = []
    sides = ((snd_dn, rcv_hi, down, 0), (snd_up, rcv_lo, up, 5))

    def exchange(stage, f, wanted):
        for j in range(len(wanted[0])):
            for side, (source, target, to, base) in enumerate(sides):
                k = wanted[side][j]
                for q in range(4):
                    source[f, k, q] = acc[f, idx[LAST_C, (base + k) * 4 + q]].astype(BF16)
                copy = pltpu.make_async_remote_copy(
                    src_ref=source.at[f, k], dst_ref=target.at[f, k],
                    send_sem=h_send.at[stage, side], recv_sem=h_recv.at[stage, side],
                    device_id={"slab": to}, device_id_type=MESH)
                copy.start()
        for side, (source, target, to, base) in enumerate(sides):
            first, count = min(wanted[side]), len(wanted[side])
            halos.append(pltpu.make_async_remote_copy(
                src_ref=source.at[f, pl.ds(first, count)], dst_ref=target.at[f, pl.ds(first, count)],
                send_sem=h_send.at[stage, side], recv_sem=h_recv.at[stage, side],
                device_id={"slab": to}, device_id_type=MESH))

    pl.semaphore_wait(barrier, len(mates))
    exchange(0, 0, ((0, 1, 2), (2, 1, 0)))
    small[5].wait()
    fill(1, cot)
    deposit(1, 0, TILES)
    exchange(1, 1, ((0, 1), (2, 1)))
    exchange(2, 1, ((2,), (0,)))

    small[3].wait()
    small[4].wait()
    lane32 = lax.broadcasted_iota(jnp.int32, (C, 128), 1) // C

    def banded(toep, flip):
        for dx in range(3):
            for zo in range(4):
                for ct in range(5):
                    tile = jnp.zeros((C, 128), F32)
                    for g in range(4):
                        dy, zi = divmod(ct * 4 + g, 6)
                        if dy < 3 and 0 <= zi - zo < 3:
                            off = 9 * (zi - zo) + 3 * dy + dx
                            off = 26 - off if flip else off
                            tile = jnp.where(lane32 == g, rep1[pl.ds(off * C, C)], tile)
                    rows = slice((dx * 4 + zo) * C, (dx * 4 + zo + 1) * C)
                    width = 128 if ct < 4 else 64
                    toep[rows, ct * 128 : ct * 128 + width] = tile[:, :width].astype(BF16)

    mixing = mix[...]
    rep1[...] = jnp.dot(
        conv[...].reshape(27 * C, C), jnp.concatenate([mixing] * 4, axis=1), preferred_element_type=F32)
    banded(toep1, False)
    mix_t = mixing.astype(F32).T.astype(BF16)

    for off in range(27):
        wide = jnp.concatenate([conv[off]] * 4, axis=0)
        rep1[off * C : (off + 1) * C] = lax.dot_general(mix_t, wide, NT, preferred_element_type=F32)
    banded(toep2, True)

    spot = lax.broadcasted_iota(jnp.int32, (128, 128), 1)
    first_x = lax.rem(spot, GX) == 0
    last_x = lax.rem(spot, GX) == GX - 1

    low_half = spot[:C] < GX

    def next_x(v):
        return jnp.where(last_x, pltpu.roll(v, GX - 1, 1), pltpu.roll(v, 127, 1))

    def prev_x(v):
        return jnp.where(first_x, pltpu.roll(v, 128 - GX + 1, 1), pltpu.roll(v, 1, 1))

    def stack(f, p):
        got = rcv_lo.at[f, p] if p < 3 else rcv_hi.at[f, p - 3]
        plane = jnp.concatenate(
            [acc[f, idx[LAST_C, (p + 1) * 4 + q]] + got[q].astype(F32) for q in range(4)], axis=1)
        own = slice(p * C, (p + 1) * C)
        shifted[f, 1, own] = plane.astype(BF16)
        turned = [pltpu.roll(plane[:, k * 128 : (k + 1) * 128], GX, 1) for k in range(16)]
        for k in range(16):
            cols = slice(k * 128, (k + 1) * 128)
            shifted[f, 0, own, cols] = jnp.where(low_half, turned[k - 1], turned[k]).astype(BF16)
            shifted[f, 2, own, cols] = jnp.where(low_half, turned[k], turned[(k + 1) % 16]).astype(BF16)

    phis = []
    win = (win0, win1)

    def convolve(f):
        toep = toep2 if f else toep1
        for q in range(4):
            cols = slice(q * TILE_C, (q + 1) * TILE_C)
            stacked = shifted[f, :, :, cols].reshape(18 * C, TILE_C)
            prod[...] = jnp.dot(toep[...], stacked, preferred_element_type=F32)
            for h in range(4):
                part = slice(h * 128, (h + 1) * 128)
                low, mid, high = (prod[d * 128 : (d + 1) * 128, part] for d in range(3))
                phi = (mid + prev_x(low) + next_x(high)).astype(BF16)
                for z in range(ZD):
                    win[f][(z + 2) * 4 + q, :, part] = phi[z * C : (z + 1) * C]
        for side, (start, land, to) in enumerate(((8, 24, down), (16, 0, up))):
            phis.append(pltpu.make_async_remote_copy(
                src_ref=win[f].at[pl.ds(start, 8)], dst_ref=win[f].at[pl.ds(land, 8)],
                send_sem=p_send.at[f, side], recv_sem=p_recv.at[f, side],
                device_id={"slab": to}, device_id_type=MESH))
            phis[-1].start()

    halos[0].wait_recv()
    halos[1].wait_recv()
    for p in range(6):
        stack(0, p)
    convolve(0)

    halos[2].wait_recv()
    halos[3].wait_recv()
    for p in range(1, 5):
        stack(1, p)
    for k in range(16):
        cols = slice(k * 128, (k + 1) * 128)
        v = shifted[1, 1, C : 5 * C, cols].astype(F32)
        for dx, moved in enumerate((next_x(v), v, prev_x(v))):
            for z in range(ZD):
                dside[z, dx * C : (dx + 1) * C, cols] = moved[z * C : (z + 1) * C].astype(BF16)
    for dy in range(3):
        total = None
        for z in range(ZD):
            part = lax.dot_general(dside[z], shifted[0, dy, z * C : (z + 3) * C], NT, preferred_element_type=F32)
            total = part if total is None else total + part
        gw[:, dy * 3 * C : (dy + 1) * 3 * C] = total
    for half in range(2):
        gp[half * 6 : (half + 1) * 6] = gw[:, half * 128 : (half + 1) * 128].reshape(6, C // 2, 128)
    gp[12:] = jnp.zeros((4, C // 2, 128), F32)
    for dx in range(3):
        gp[12:14, :, dx * C : (dx + 1) * C] = gw[dx * C : (dx + 1) * C, 256:].reshape(2, C // 2, C)

    def give(source, target, phase, mate):
        pltpu.make_async_remote_copy(
            src_ref=source, dst_ref=target, send_sem=g_send.at[phase], recv_sem=g_recv.at[phase],
            device_id=mate, device_id_type=MESH).start()

    def all_of(buffer, count, phase):
        part = buffer.at[pl.ds(0, count)]
        return pltpu.make_async_remote_copy(
            src_ref=part, dst_ref=part, send_sem=g_send.at[phase], recv_sem=g_recv.at[phase],
            device_id=plane_mates[0], device_id_type=MESH)

    for k in range(1, GROUP):
        give(gp.at[lax.rem(member + k, GROUP)], rs1.at[k], 0, plane_mates[k - 1])
    rs1[0] = gp[member]

    halos[4].wait_recv()
    halos[5].wait_recv()
    stack(1, 0)
    stack(1, 5)
    convolve(1)

    all_of(rs1, GROUP - 1, 0).wait_recv()
    piece[...] = jnp.sum(rs1[...], axis=0)
    for k in range(1, ROW):
        give(piece, rs2.at[chip], 1, row_mates[k - 1])
    rs2[chip] = piece[...]

    def collect(f):
        def body(i, carry):
            first = i * UNROLL
            values = [lax.dot_general(win[f][idx[CELL, first + u]], w[first + u], NT, preferred_element_type=F32)
                      for u in range(UNROLL)]
            for u in range(UNROLL):
                cacc[f, first + u + 1] = values[u] + cacc[f, idx[PREV_A, first + u]]
            return carry

        lax.fori_loop(0, TILES // UNROLL, body, 0)
        out_v, out = (gfe_v, gfe) if f else (pot_v, pot)
        for a in range(0, NAB, 2):
            pair = jnp.concatenate([cacc[f, idx[LAST_A, a]], cacc[f, idx[LAST_A, a + 1]]], axis=1)
            out_v[:, a * TILE_A : (a + 2) * TILE_A] = pair.astype(BF16)
        copy = pltpu.make_async_copy(out_v, out, out_sem.at[f])
        copy.start()
        return copy

    phis[0].wait_recv()
    phis[1].wait_recv()
    outs = [collect(0)]

    all_of(rs2, ROW - 1, 1).wait_recv()
    fin[...] = jnp.sum(rs2[...], axis=0)
    for k in range(1, GROUP):
        give(fin, gout.at[member], 2, plane_mates[k - 1])
    outs.append(pltpu.make_async_copy(fin, gout.at[member], out_sem.at[2]))
    outs[-1].start()

    phis[2].wait_recv()
    phis[3].wait_recv()
    outs.append(collect(1))

    all_of(rs1, GROUP - 1, 0).wait_send()
    all_of(rs2, ROW - 1, 1).wait_send()
    for copy in halos + phis:
        copy.wait_send()
    all_of(rs1, GROUP - 1, 2).wait_send()
    all_of(rs1, GROUP - 1, 2).wait_recv()
    for copy in outs:
        copy.wait()


def finish(pot_in, gfe_in, moments_hbm, mix_hbm, conv_hbm, pot, gfe, gconv, gmix, moments, mix, conv, flat, sem):
    pairs = ((moments_hbm, moments), (mix_hbm, mix), (conv_hbm, conv), (pot_in, pot), (gfe_in, gfe))
    copies = [pltpu.make_async_copy(source, target, sem.at[k]) for k, (source, target) in enumerate(pairs)]
    for copy in copies:
        copy.start()
    for copy in copies[:3]:
        copy.wait()
    for off in range(27):
        dz, dy, dx = off // 9, off // 3 % 3, off % 3
        group = dy * 3 + dz
        first, place = (group // 4 * 6 + dx * 2, group % 4) if group < 8 else (12, dx)
        part = moments[first : first + 2, :, place * C : (place + 1) * C]
        flat[off * C : (off + 1) * C] = part.reshape(C, C)
    value = flat[...]
    high = value.astype(BF16)
    low = (value - high.astype(F32)).astype(BF16)
    mixing = mix[...]
    turned = conv[...].reshape(27 * C, C).astype(F32).T.astype(BF16)
    devices = REPS * SLABS
    conv_scale = 1.0 / math.sqrt(devices * ZD * GY * GX)
    mix_scale = 1.0 / math.sqrt(devices * A_DEV)
    product = (lax.dot_general(high, mixing, NT, preferred_element_type=F32)
               + lax.dot_general(low, mixing, NT, preferred_element_type=F32))
    gconv[...] = (product * conv_scale).reshape(27, C, C)
    gmix[...] = (jnp.dot(turned, high, preferred_element_type=F32)
                 + jnp.dot(turned, low, preferred_element_type=F32)) * mix_scale
    for copy in copies[3:]:
        copy.wait()


def local(feats, tile_weight, tile_atom, tile_cell, tile_live, w_mix, conv_w, cotangent):
    vmem = pl.BlockSpec(memory_space=pltpu.VMEM)
    hbm = pl.BlockSpec(memory_space=pltpu.HBM)
    dma = pltpu.SemaphoreType.DMA
    field = jax.ShapeDtypeStruct((C, A_DEV), BF16)
    pot, gfe, total = pl.pallas_call(
        kernel,
        out_shape=(field, field, jax.ShapeDtypeStruct((GROUP, C // 2, 128), F32)),
        in_specs=[hbm] * 4 + [pl.BlockSpec(memory_space=pltpu.SMEM)] + [hbm] * 3,
        out_specs=(hbm, hbm, hbm),
        scratch_shapes=[
            pltpu.VMEM((C, A_DEV), BF16),
            pltpu.VMEM((C, A_DEV), BF16),
            pltpu.VMEM((C, A_DEV), BF16),
            pltpu.VMEM((C, A_DEV), BF16),
            pltpu.VMEM((27, C, C), BF16),
            pltpu.VMEM((C, C), BF16),
            pltpu.VMEM((1, TILES), jnp.int32),
            pltpu.VMEM((1, TILES), jnp.int32),
            pltpu.VMEM((8, 128), jnp.int32),
            pltpu.SMEM((8, 128), jnp.int32),
            pltpu.VMEM((TILES, TILE_A, TILE_C), BF16),
            pltpu.VMEM((2, NAB, C, TILE_A), BF16),
            pltpu.VMEM((2, TILES + 1, C, TILE_C), F32),
            pltpu.VMEM((2, 3, 4, C, TILE_C), BF16),
            pltpu.VMEM((2, 3, 4, C, TILE_C), BF16),
            pltpu.VMEM((2, 3, 4, C, TILE_C), BF16),
            pltpu.VMEM((2, 3, 4, C, TILE_C), BF16),
            pltpu.VMEM((2, 3, 6 * C, CELLS), BF16),
            pltpu.VMEM((ZD, 3 * C, CELLS), BF16),
            pltpu.VMEM((12 * C, 18 * C), BF16),
            pltpu.VMEM((12 * C, 18 * C), BF16),
            pltpu.VMEM((27 * C, 128), F32),
            pltpu.VMEM((12 * C, TILE_C), F32),
            pltpu.VMEM((3 * C, 9 * C), F32),
            pltpu.VMEM((NB, C, TILE_C), BF16),
            pltpu.VMEM((NB, C, TILE_C), BF16),
            pltpu.VMEM((2, TILES + 1, C, TILE_A), F32),
            pltpu.VMEM((GROUP, C // 2, 128), F32),
            pltpu.VMEM((GROUP, C // 2, 128), F32),
            pltpu.VMEM((ROW, C // 2, 128), F32),
            pltpu.VMEM((C // 2, 128), F32),
            pltpu.VMEM((C // 2, 128), F32),
            dma((7,)), dma((3,)), dma((W_CHUNKS,)), dma((3, 2)), dma((3, 2)), dma((2, 2)), dma((2, 2)), dma((3,)), dma((3,)),
        ],
        compiler_params=pltpu.CompilerParams(
            collective_id=0, has_side_effects=True, vmem_limit_bytes=56 * 2**20,
        ),
    )(feats[0], tile_weight[0], tile_atom, tile_cell, tile_live, w_mix, conv_w, cotangent[0])
    pot, gfe, gconv, gmix = pl.pallas_call(
        finish,
        out_shape=(field, field, jax.ShapeDtypeStruct((27, C, C), F32), jax.ShapeDtypeStruct((C, C), F32)),
        in_specs=[hbm] * 5,
        out_specs=(vmem,) * 4,
        scratch_shapes=[
            pltpu.VMEM((GROUP, C // 2, 128), F32),
            pltpu.VMEM((C, C), BF16),
            pltpu.VMEM((27, C, C), BF16),
            pltpu.VMEM((27 * C, C), F32),
            dma((5,)),
        ],
    )(pot, gfe, total, w_mix, conv_w)
    return pot[None], gfe[None], gconv, gmix


def solution(mesh):
    return jax.shard_map(
        local,
        mesh=mesh,
        in_specs=(
            P("rep", None, "slab"),
            P("rep", "slab", None, None),
            P("rep", "slab"),
            P("rep", "slab"),
            P("rep", "slab"),
            P(),
            P(),
            P("rep", None, "slab"),
        ),
        out_specs=(P("rep", None, "slab"), P("rep", None, "slab"), P(), P()),
        check_vma=False,
    )
```

```python
import math

import jax
import jax.numpy as jnp
from jax import lax
from jax.experimental import pallas as pl
from jax.experimental.pallas import tpu as pltpu
from jax.sharding import PartitionSpec as P

C = 32
GY = 32
GX = 64
ZD = 4
A_DEV = 1536
TILES = 96
TILE_A = 64
TILE_C = 512
NB = 32
NAB = 24
CELLS = GY * GX
SLABS = 16
REPS = 8
W_CHUNKS = 4
W_STEP = TILES // W_CHUNKS

UNROLL = 24
GROUP = 16
ROW = 8
GROUP_STEPS = (10, 11, 9, 8, 6, 14, 7, 5, 13, 15, 4, 12, 3, 2, 1)
ROW_STEPS = (6, 2, 5, 3, 7, 1, 4)
PREV_C, LAST_C, PREV_A, LAST_A, ATOM, CELL = range(6)

F32 = jnp.float32
BF16 = jnp.bfloat16
NT = (((1,), (1,)), ((), ()))
MESH = pl.DeviceIdType.MESH


def kernel(
    feats_hbm, w_hbm, atom_hbm, cell_hbm, live, mix_hbm, conv_hbm, cot_hbm,
    pot, gfe, gout,
    pot_v, gfe_v, feats, cot, conv, mix, atom_v, cell_v, idx_v, idx,
    w, src, acc, snd_dn, snd_up, rcv_lo, rcv_hi, shifted, dside, toep1, toep2, rep1, prod, gw,
    win0, win1, cacc, gp, rs1, rs2, piece, fin,
    in_sem, out_sem, w_sem, h_send, h_recv, p_send, p_recv, g_send, g_recv,
):
    slab = lax.axis_index("slab")
    rep = lax.axis_index("rep")
    chip, core = slab // 2, lax.rem(slab, 2)
    member = rep * 2 + core
    up = lax.rem(slab + 1, SLABS)
    down = lax.rem(slab + SLABS - 1, SLABS)

    small = []
    pairs = ((cell_hbm, cell_v), (atom_hbm, atom_v), (feats_hbm, feats), (mix_hbm, mix),
             (conv_hbm, conv), (cot_hbm, cot))
    for k, (source, target) in enumerate(pairs):
        small.append(pltpu.make_async_copy(source, target, in_sem.at[k]))
        small[-1].start()
    loads = []
    for k in range(W_CHUNKS):
        part = pl.ds(k * W_STEP, W_STEP)
        loads.append(pltpu.make_async_copy(w_hbm.at[part], w.at[part], w_sem.at[k]))
        loads[-1].start()

    def plane_mate(k):
        other = lax.rem(member + k, GROUP)
        return {"rep": other // 2, "slab": chip * 2 + lax.rem(other, 2)}

    def row_mate(k):
        return {"slab": lax.rem(chip + k, ROW) * 2 + core}

    plane_mates = [plane_mate(k) for k in range(1, GROUP)]
    row_mates = [row_mate(k) for k in range(1, ROW)]
    mates = plane_mates + row_mates + [{"slab": up}, {"slab": down}]
    barrier = pltpu.get_barrier_semaphore()
    for mate in mates:
        pl.semaphore_signal(barrier, inc=1, device_id=mate, device_id_type=MESH)

    small[0].wait()
    small[1].wait()
    lane = lax.broadcasted_iota(jnp.int32, (TILES, TILES), 1)
    sub = lax.broadcasted_iota(jnp.int32, (TILES, TILES), 0)
    alive = sub < live[0, 0]
    number = sub + 1
    for ids, prev, last, copied, limit in (
        (cell_v, PREV_C, LAST_C, CELL, NB - 1), (atom_v, PREV_A, LAST_A, ATOM, NAB - 1)
    ):
        row = jnp.broadcast_to(ids[...], (TILES, TILES))
        column = jnp.sum(jnp.where(lane == sub, row, 0), axis=1, keepdims=True)
        before = jnp.where((column == row) & (sub < lane) & alive, number, 0)
        newest = jnp.where((column == lane) & alive, number, 0)
        idx_v[prev : prev + 1, :TILES] = jnp.clip(jnp.max(before, axis=0, keepdims=True), 0, TILES)
        idx_v[last : last + 1, :TILES] = jnp.clip(jnp.max(newest, axis=0, keepdims=True), 0, TILES)
        idx_v[copied : copied + 1, :TILES] = jnp.clip(ids[...], 0, limit)
    table = pltpu.make_async_copy(idx_v, idx, in_sem.at[6])
    table.start()

    def fill(f, values):
        for a in range(NAB):
            src[f, a] = values[:, a * TILE_A : (a + 1) * TILE_A]
        acc[f, 0] = jnp.zeros((C, TILE_C), F32)
        cacc[f, 0] = jnp.zeros((C, TILE_A), F32)

    small[2].wait()
    fill(0, feats)
    table.wait()

    def deposit(f, start, stop):
        def body(i, carry):
            first = i * UNROLL
            values = [jnp.dot(src[f, idx[ATOM, first + u]], w[first + u], preferred_element_type=F32)
                      for u in range(UNROLL)]
            for u in range(UNROLL):
                acc[f, first + u + 1] = values[u] + acc[f, idx[PREV_C, first + u]]
            return carry

        lax.fori_loop(start // UNROLL, stop // UNROLL, body, 0)

    for k in range(W_CHUNKS):
        loads[k].wait()
        deposit(0, k * W_STEP, (k + 1) * W_STEP)

    halos = []
    sides = ((snd_dn, rcv_hi, down, 0), (snd_up, rcv_lo, up, 5))

    def exchange(stage, f, wanted):
        for j in range(len(wanted[0])):
            for side, (source, target, to, base) in enumerate(sides):
                k = wanted[side][j]
                for q in range(4):
                    source[f, k, q] = acc[f, idx[LAST_C, (base + k) * 4 + q]].astype(BF16)
                copy = pltpu.make_async_remote_copy(
                    src_ref=source.at[f, k], dst_ref=target.at[f, k],
                    send_sem=h_send.at[stage, side], recv_sem=h_recv.at[stage, side],
                    device_id={"slab": to}, device_id_type=MESH)
                copy.start()
        for side, (source, target, to, base) in enumerate(sides):
            first, count = min(wanted[side]), len(wanted[side])
            halos.append(pltpu.make_async_remote_copy(
                src_ref=source.at[f, pl.ds(first, count)], dst_ref=target.at[f, pl.ds(first, count)],
                send_sem=h_send.at[stage, side], recv_sem=h_recv.at[stage, side],
                device_id={"slab": to}, device_id_type=MESH))

    pl.semaphore_wait(barrier, len(mates))
    exchange(0, 0, ((0, 1, 2), (2, 1, 0)))
    small[5].wait()
    fill(1, cot)
    deposit(1, 0, TILES)
    exchange(1, 1, ((0, 1), (2, 1)))
    exchange(2, 1, ((2,), (0,)))

    small[3].wait()
    small[4].wait()
    lane32 = lax.broadcasted_iota(jnp.int32, (C, 128), 1) // C

    def banded(toep, flip):
        for dx in range(3):
            for zo in range(4):
                for ct in range(5):
                    tile = jnp.zeros((C, 128), F32)
                    for g in range(4):
                        dy, zi = divmod(ct * 4 + g, 6)
                        if dy < 3 and 0 <= zi - zo < 3:
                            off = 9 * (zi - zo) + 3 * dy + dx
                            off = 26 - off if flip else off
                            tile = jnp.where(lane32 == g, rep1[pl.ds(off * C, C)], tile)
                    rows = slice((dx * 4 + zo) * C, (dx * 4 + zo + 1) * C)
                    width = 128 if ct < 4 else 64
                    toep[rows, ct * 128 : ct * 128 + width] = tile[:, :width].astype(BF16)

    mixing = mix[...]
    rep1[...] = jnp.dot(
        conv[...].reshape(27 * C, C), jnp.concatenate([mixing] * 4, axis=1), preferred_element_type=F32)
    banded(toep1, False)
    mix_t = mixing.astype(F32).T.astype(BF16)

    for off in range(27):
        wide = jnp.concatenate([conv[off]] * 4, axis=0)
        rep1[off * C : (off + 1) * C] = lax.dot_general(mix_t, wide, NT, preferred_element_type=F32)
    banded(toep2, True)

    spot = lax.broadcasted_iota(jnp.int32, (128, 128), 1)
    first_x = lax.rem(spot, GX) == 0
    last_x = lax.rem(spot, GX) == GX - 1

    low_half = spot[:C] < GX

    def next_x(v):
        return jnp.where(last_x, pltpu.roll(v, GX - 1, 1), pltpu.roll(v, 127, 1))

    def prev_x(v):
        return jnp.where(first_x, pltpu.roll(v, 128 - GX + 1, 1), pltpu.roll(v, 1, 1))

    def stack(f, p):
        got = rcv_lo.at[f, p] if p < 3 else rcv_hi.at[f, p - 3]
        plane = jnp.concatenate(
            [acc[f, idx[LAST_C, (p + 1) * 4 + q]] + got[q].astype(F32) for q in range(4)], axis=1)
        own = slice(p * C, (p + 1) * C)
        shifted[f, 1, own] = plane.astype(BF16)
        turned = [pltpu.roll(plane[:, k * 128 : (k + 1) * 128], GX, 1) for k in range(16)]
        for k in range(16):
            cols = slice(k * 128, (k + 1) * 128)
            shifted[f, 0, own, cols] = jnp.where(low_half, turned[k - 1], turned[k]).astype(BF16)
            shifted[f, 2, own, cols] = jnp.where(low_half, turned[k], turned[(k + 1) % 16]).astype(BF16)

    phis = []
    win = (win0, win1)

    def convolve(f):
        toep = toep2 if f else toep1
        for q in range(4):
            cols = slice(q * TILE_C, (q + 1) * TILE_C)
            stacked = shifted[f, :, :, cols].reshape(18 * C, TILE_C)
            prod[...] = jnp.dot(toep[...], stacked, preferred_element_type=F32)
            for h in range(4):
                part = slice(h * 128, (h + 1) * 128)
                low, mid, high = (prod[d * 128 : (d + 1) * 128, part] for d in range(3))
                phi = (mid + prev_x(low) + next_x(high)).astype(BF16)
                for z in range(ZD):
                    win[f][(z + 2) * 4 + q, :, part] = phi[z * C : (z + 1) * C]
        for side, (start, land, to) in enumerate(((8, 24, down), (16, 0, up))):
            phis.append(pltpu.make_async_remote_copy(
                src_ref=win[f].at[pl.ds(start, 8)], dst_ref=win[f].at[pl.ds(land, 8)],
                send_sem=p_send.at[f, side], recv_sem=p_recv.at[f, side],
                device_id={"slab": to}, device_id_type=MESH))
            phis[-1].start()

    halos[0].wait_recv()
    halos[1].wait_recv()
    for p in range(6):
        stack(0, p)
    convolve(0)

    halos[2].wait_recv()
    halos[3].wait_recv()
    for p in range(1, 5):
        stack(1, p)
    for k in range(16):
        cols = slice(k * 128, (k + 1) * 128)
        v = shifted[1, 1, C : 5 * C, cols].astype(F32)
        for dx, moved in enumerate((next_x(v), v, prev_x(v))):
            for z in range(ZD):
                dside[z, dx * C : (dx + 1) * C, cols] = moved[z * C : (z + 1) * C].astype(BF16)
    for dy in range(3):
        total = None
        for z in range(ZD):
            part = lax.dot_general(dside[z], shifted[0, dy, z * C : (z + 3) * C], NT, preferred_element_type=F32)
            total = part if total is None else total + part
        gw[:, dy * 3 * C : (dy + 1) * 3 * C] = total
    for half in range(2):
        gp[half * 6 : (half + 1) * 6] = gw[:, half * 128 : (half + 1) * 128].reshape(6, C // 2, 128)
    gp[12:] = jnp.zeros((4, C // 2, 128), F32)
    for dx in range(3):
        gp[12:14, :, dx * C : (dx + 1) * C] = gw[dx * C : (dx + 1) * C, 256:].reshape(2, C // 2, C)

    def give(source, target, phase, mate):
        pltpu.make_async_remote_copy(
            src_ref=source, dst_ref=target, send_sem=g_send.at[phase], recv_sem=g_recv.at[phase],
            device_id=mate, device_id_type=MESH).start()

    def all_of(buffer, count, phase):
        part = buffer.at[pl.ds(0, count)]
        return pltpu.make_async_remote_copy(
            src_ref=part, dst_ref=part, send_sem=g_send.at[phase], recv_sem=g_recv.at[phase],
            device_id=plane_mates[0], device_id_type=MESH)

    for k in GROUP_STEPS:
        give(gp.at[lax.rem(member + k, GROUP)], rs1.at[k], 0, plane_mates[k - 1])
    rs1[0] = gp[member]

    halos[4].wait_recv()
    halos[5].wait_recv()
    stack(1, 0)
    stack(1, 5)
    convolve(1)

    all_of(rs1, GROUP - 1, 0).wait_recv()
    piece[...] = jnp.sum(rs1[...], axis=0)
    for k in ROW_STEPS:
        give(piece, rs2.at[chip], 1, row_mates[k - 1])
    rs2[chip] = piece[...]

    def collect(f):
        def body(i, carry):
            first = i * UNROLL
            values = [lax.dot_general(win[f][idx[CELL, first + u]], w[first + u], NT, preferred_element_type=F32)
                      for u in range(UNROLL)]
            for u in range(UNROLL):
                cacc[f, first + u + 1] = values[u] + cacc[f, idx[PREV_A, first + u]]
            return carry

        lax.fori_loop(0, TILES // UNROLL, body, 0)
        out_v, out = (gfe_v, gfe) if f else (pot_v, pot)
        for a in range(0, NAB, 2):
            pair = jnp.concatenate([cacc[f, idx[LAST_A, a]], cacc[f, idx[LAST_A, a + 1]]], axis=1)
            out_v[:, a * TILE_A : (a + 2) * TILE_A] = pair.astype(BF16)
        copy = pltpu.make_async_copy(out_v, out, out_sem.at[f])
        copy.start()
        return copy

    phis[0].wait_recv()
    phis[1].wait_recv()
    outs = [collect(0)]

    all_of(rs2, ROW - 1, 1).wait_recv()
    fin[...] = jnp.sum(rs2[...], axis=0)
    for k in GROUP_STEPS:
        give(fin, gout.at[member], 2, plane_mates[k - 1])
    outs.append(pltpu.make_async_copy(fin, gout.at[member], out_sem.at[2]))
    outs[-1].start()

    phis[2].wait_recv()
    phis[3].wait_recv()
    outs.append(collect(1))

    all_of(rs1, GROUP - 1, 0).wait_send()
    all_of(rs2, ROW - 1, 1).wait_send()
    for copy in halos + phis:
        copy.wait_send()
    all_of(rs1, GROUP - 1, 2).wait_send()
    all_of(rs1, GROUP - 1, 2).wait_recv()
    for copy in outs:
        copy.wait()


def finish(pot_in, gfe_in, moments_hbm, mix_hbm, conv_hbm, pot, gfe, gconv, gmix, moments, mix, conv, flat, sem):
    pairs = ((moments_hbm, moments), (mix_hbm, mix), (conv_hbm, conv), (pot_in, pot), (gfe_in, gfe))
    copies = [pltpu.make_async_copy(source, target, sem.at[k]) for k, (source, target) in enumerate(pairs)]
    for copy in copies:
        copy.start()
    copies[1].wait()
    copies[2].wait()
    mixing = mix[...]
    turned = conv[...].reshape(27 * C, C).astype(F32).T.astype(BF16)
    copies[0].wait()
    for off in range(27):
        dz, dy, dx = off // 9, off // 3 % 3, off % 3
        group = dy * 3 + dz
        first, place = (group // 4 * 6 + dx * 2, group % 4) if group < 8 else (12, dx)
        part = moments[first : first + 2, :, place * C : (place + 1) * C]
        flat[off * C : (off + 1) * C] = part.reshape(C, C)
    value = flat[...]
    high = value.astype(BF16)
    low = (value - high.astype(F32)).astype(BF16)
    devices = REPS * SLABS
    conv_scale = 1.0 / math.sqrt(devices * ZD * GY * GX)
    mix_scale = 1.0 / math.sqrt(devices * A_DEV)
    product = (lax.dot_general(high, mixing, NT, preferred_element_type=F32)
               + lax.dot_general(low, mixing, NT, preferred_element_type=F32))
    gconv[...] = (product * conv_scale).reshape(27, C, C)
    gmix[...] = (jnp.dot(turned, high, preferred_element_type=F32)
                 + jnp.dot(turned, low, preferred_element_type=F32)) * mix_scale
    for copy in copies[3:]:
        copy.wait()


def local(feats, tile_weight, tile_atom, tile_cell, tile_live, w_mix, conv_w, cotangent):
    vmem = pl.BlockSpec(memory_space=pltpu.VMEM)
    hbm = pl.BlockSpec(memory_space=pltpu.HBM)
    dma = pltpu.SemaphoreType.DMA
    field = jax.ShapeDtypeStruct((C, A_DEV), BF16)
    pot, gfe, total = pl.pallas_call(
        kernel,
        out_shape=(field, field, jax.ShapeDtypeStruct((GROUP, C // 2, 128), F32)),
        in_specs=[hbm] * 4 + [pl.BlockSpec(memory_space=pltpu.SMEM)] + [hbm] * 3,
        out_specs=(hbm, hbm, hbm),
        scratch_shapes=[
            pltpu.VMEM((C, A_DEV), BF16),
            pltpu.VMEM((C, A_DEV), BF16),
            pltpu.VMEM((C, A_DEV), BF16),
            pltpu.VMEM((C, A_DEV), BF16),
            pltpu.VMEM((27, C, C), BF16),
            pltpu.VMEM((C, C), BF16),
            pltpu.VMEM((1, TILES), jnp.int32),
            pltpu.VMEM((1, TILES), jnp.int32),
            pltpu.VMEM((8, 128), jnp.int32),
            pltpu.SMEM((8, 128), jnp.int32),
            pltpu.VMEM((TILES, TILE_A, TILE_C), BF16),
            pltpu.VMEM((2, NAB, C, TILE_A), BF16),
            pltpu.VMEM((2, TILES + 1, C, TILE_C), F32),
            pltpu.VMEM((2, 3, 4, C, TILE_C), BF16),
            pltpu.VMEM((2, 3, 4, C, TILE_C), BF16),
            pltpu.VMEM((2, 3, 4, C, TILE_C), BF16),
            pltpu.VMEM((2, 3, 4, C, TILE_C), BF16),
            pltpu.VMEM((2, 3, 6 * C, CELLS), BF16),
            pltpu.VMEM((ZD, 3 * C, CELLS), BF16),
            pltpu.VMEM((12 * C, 18 * C), BF16),
            pltpu.VMEM((12 * C, 18 * C), BF16),
            pltpu.VMEM((27 * C, 128), F32),
            pltpu.VMEM((12 * C, TILE_C), F32),
            pltpu.VMEM((3 * C, 9 * C), F32),
            pltpu.VMEM((NB, C, TILE_C), BF16),
            pltpu.VMEM((NB, C, TILE_C), BF16),
            pltpu.VMEM((2, TILES + 1, C, TILE_A), F32),
            pltpu.VMEM((GROUP, C // 2, 128), F32),
            pltpu.VMEM((GROUP, C // 2, 128), F32),
            pltpu.VMEM((ROW, C // 2, 128), F32),
            pltpu.VMEM((C // 2, 128), F32),
            pltpu.VMEM((C // 2, 128), F32),
            dma((7,)), dma((3,)), dma((W_CHUNKS,)), dma((3, 2)), dma((3, 2)), dma((2, 2)), dma((2, 2)), dma((3,)), dma((3,)),
        ],
        compiler_params=pltpu.CompilerParams(
            collective_id=0, has_side_effects=True, vmem_limit_bytes=56 * 2**20,
        ),
    )(feats[0], tile_weight[0], tile_atom, tile_cell, tile_live, w_mix, conv_w, cotangent[0])
    pot, gfe, gconv, gmix = pl.pallas_call(
        finish,
        out_shape=(field, field, jax.ShapeDtypeStruct((27, C, C), F32), jax.ShapeDtypeStruct((C, C), F32)),
        in_specs=[hbm] * 5,
        out_specs=(vmem,) * 4,
        scratch_shapes=[
            pltpu.VMEM((GROUP, C // 2, 128), F32),
            pltpu.VMEM((C, C), BF16),
            pltpu.VMEM((27, C, C), BF16),
            pltpu.VMEM((27 * C, C), F32),
            dma((5,)),
        ],
    )(pot, gfe, total, w_mix, conv_w)
    return pot[None], gfe[None], gconv, gmix


def solution(mesh):
    return jax.shard_map(
        local,
        mesh=mesh,
        in_specs=(
            P("rep", None, "slab"),
            P("rep", "slab", None, None),
            P("rep", "slab"),
            P("rep", "slab"),
            P("rep", "slab"),
            P(),
            P(),
            P("rep", None, "slab"),
        ),
        out_specs=(P("rep", None, "slab"), P("rep", None, "slab"), P(), P()),
        check_vma=False,
    )
```
